512 devices in a mesh: dp: 32 (over z_hi, x, core), fsdp: 16 (over y, z_lo).
Axes of the slice: x: 4, y: 8, z: 8 (z_hi: 4, z_lo: 2; z = z_hi * 2 + z_lo), core: 2. Of those that a mesh axis runs over, the one named last changes fastest.
Arguments:
- tokens: bfloat16 [4096, 8192], P('dp', 'fsdp'), may hold values from -6 to 6
- cotangent: bfloat16 [4096, 4096], P('dp', 'fsdp'), may hold values from -6 to 6
- blocks: bfloat16 [1024, 128, 128], P('fsdp'), may hold values from -0.125 to 0.125
- slot_block: int32 [1024], P('fsdp'), may hold values from 0 to 2047, as said below
- shard_count: int32 [16], P('fsdp'), may hold values from 1 to 64, 512 in all
Outputs:
- projected: bfloat16 [4096, 4096], P('dp', 'fsdp')
- input_grad: bfloat16 [4096, 8192], P('dp', 'fsdp')
- block_grad: bfloat16 [1024, 128, 128], P('fsdp')
The draws below stay inside these ranges and needn't reach their ends.
Inputs may be any that keep to these rules, and one draw needn't show every extreme that they name: The first shard_count[q] slots of group q are its live slots; the entries sum to 512. `slot_block`: all entries are distinct; the block of slot s has its column c in the band of group s // 64, that is c * 16 // 32 == s // 64.
All inputs are finite; a program needn't handle non-finite values.
Results may differ from the reference program's by a relative error of at most 0.001.
Values may be sent and summed in bfloat16 or wider, within the bound.
A program may use at most 128 MiB of HBM per device.

```python
import math
import jax
import jax.numpy as jnp
import numpy as np
from jax import lax

DIN = 8192
DOUT = 4096
BLK = 128
TOKENS = 4096
NNZ = 512
CAP = 64
N_FSDP = 16


def draw_slot_block(key, part):
    n_out = DOUT // BLK
    per_band = n_out // N_FSDP
    band_size = DIN // BLK * per_band

    def one_band(band_idx):
        order = jax.random.permutation(jax.random.fold_in(key, band_idx), band_size)[:CAP]
        row_ids = order // per_band
        col_ids = band_idx * per_band + order % per_band
        return (row_ids * n_out + col_ids).astype(jnp.int32)
    return jax.vmap(one_band)(jnp.arange(N_FSDP, dtype=jnp.int32)).reshape(-1)


def level_of(key, shape, cuts, least, largest):
    factor_of, own = 1.0, jax.random.fold_in(key, 6)
    for dim, parts in cuts:
        steps = jnp.exp(jax.random.uniform(jax.random.fold_in(own, dim), (parts,), jnp.float32, least / len(cuts), largest / len(cuts)))
        factor_of = factor_of * jnp.repeat(steps, shape[dim] // parts).reshape([-1 if axis == dim else 1 for axis in range(len(shape))])
    return factor_of


def split_up(number_of, total, reach, skew):
    loads = [(1 << 20) // math.isqrt(grade ** skew) + 1 for grade in range(2, number_of + 1)]
    surplus, counts = total - reach - (number_of - 1), [1] * (number_of - 1)
    while surplus > 0:
        candidates = [i for i in range(number_of - 1) if counts[i] < reach]
        whole, left = sum([loads[i] for i in candidates]), surplus
        for i in candidates:
            addition = min(reach - counts[i], max(1, left * loads[i] // whole), surplus)
            counts[i] = counts[i] + addition
            surplus = surplus - addition
    return np.array([reach] + counts)


def ragged_sizes(stream_key, amount, total, bound, lean):
    if amount == 2:
        one = jax.random.randint(stream_key, (), max(1, total - bound), min(bound, total - 1) + 1)
        return jnp.stack([one, total - one])
    sizes = jnp.asarray(split_up(amount, total, bound, lean), jnp.int32)
    pairs = (amount - 1) // 2
    source_of, receiver = sizes[1:1 + 2 * pairs:2], sizes[2:2 + 2 * pairs:2]
    margin = jnp.minimum(source_of - 1, bound - receiver)
    moved = jax.random.randint(jax.random.fold_in(stream_key, 1), (pairs,), 0, 1 << 20) % (margin + 1)
    sizes = sizes.at[1:1 + 2 * pairs:2].set(source_of - moved).at[2:2 + 2 * pairs:2].set(receiver + moved)
    return sizes[jax.random.permutation(jax.random.fold_in(stream_key, 2), amount)]


def scatter_about(rng, dims, spread, limit, shards=(), kind=jnp.bfloat16):
    level = level_of(rng, dims, shards, -0.22, 0.18) if shards else 1.0
    drawn = jax.random.normal(rng, dims, jnp.float32) * spread * level
    return jnp.minimum(jnp.maximum(drawn, -limit), limit).astype(kind)


def setup_inputs(seed: int = 0) -> dict:
    key_list = jax.random.split(jax.random.key(seed), 6)
    tokens = scatter_about(key_list[0], (TOKENS, DIN), 1.0, 6.0, ((0, 32), (1, 16)))
    cotangent = scatter_about(key_list[1], (TOKENS, DOUT), 1.0, 6.0, ((0, 32), (1, 16)))
    blocks = scatter_about(key_list[2], (N_FSDP * CAP, BLK, BLK), (DIN // 4) ** -0.5, 0.125, ((0, 16),))
    slot_block = draw_slot_block(jax.random.fold_in(key_list[5], 71), 0)
    shard_count = ragged_sizes(key_list[4], N_FSDP, NNZ, CAP, 2).astype(jnp.int32)
    return {"tokens": tokens, "cotangent": cotangent, "blocks": blocks, "slot_block": slot_block, "shard_count": shard_count}


def reference(tokens, cotangent, blocks, slot_block, shard_count):
    n_in = DIN // BLK
    n_out = DOUT // BLK
    x_blocks = tokens.astype(jnp.float32).reshape(TOKENS, n_in, BLK)
    g_blocks = cotangent.astype(jnp.float32).reshape(TOKENS, n_out, BLK)
    slot_ids = slot_block.reshape(N_FSDP, CAP)
    weights = blocks.reshape(N_FSDP, CAP, BLK, BLK)
    position = jnp.arange(CAP, dtype=jnp.int32)
    highest = lax.Precision.HIGHEST

    def one_shard(carry, inputs):
        y_sum, dx_sum = carry
        ids_shard, w_shard, count_shard = inputs
        live_mask = (position < count_shard).astype(jnp.float32)
        w_live = w_shard.astype(jnp.float32) * live_mask[:, None, None]
        row_ids = (ids_shard // n_out).astype(jnp.int32)
        col_ids = (ids_shard % n_out).astype(jnp.int32)
        x_cols = jnp.take(x_blocks, row_ids, axis=1)
        g_cols = jnp.take(g_blocks, col_ids, axis=1)
        out_onehot = (col_ids[:, None] == jnp.arange(n_out, dtype=jnp.int32)[None, :]).astype(jnp.float32)
        in_onehot = (row_ids[:, None] == jnp.arange(n_in, dtype=jnp.int32)[None, :]).astype(jnp.float32)
        y_terms = jnp.einsum("tsk,skn->tsn", x_cols, w_live, precision=highest)
        y_part = jnp.einsum("tsn,sj->tjn", y_terms, out_onehot, precision=highest)
        dx_terms = jnp.einsum("tsn,skn->tsk", g_cols, w_live, precision=highest)
        dx_part = jnp.einsum("tsk,si->tik", dx_terms, in_onehot, precision=highest)
        dw_shard = jnp.einsum("tsk,tsn->skn", x_cols, g_cols, precision=highest) * live_mask[:, None, None]
        return (y_sum + y_part, dx_sum + dx_part), dw_shard

    start = (jnp.zeros((TOKENS, n_out, BLK), jnp.float32), jnp.zeros((TOKENS, n_in, BLK), jnp.float32))
    (y_sum, dx_sum), dw_all = lax.scan(one_shard, start, (slot_ids, weights, shard_count))
    projected = y_sum.reshape(TOKENS, DOUT).astype(jnp.bfloat16)
    input_grad = dx_sum.reshape(TOKENS, DIN).astype(jnp.bfloat16)
    block_grad = dw_all.reshape(N_FSDP * CAP, BLK, BLK).astype(jnp.bfloat16)
    return projected, input_grad, block_grad
```

```python
import functools

import jax
import jax.numpy as jnp
from jax import lax
from jax.experimental import pallas as pl
from jax.experimental.pallas import tpu as pltpu
from jax.sharding import PartitionSpec as P

BLK = 128
NY, NZL, NX, NZH = 8, 2, 4, 4
TOK = 128
XF = 512
CF = 256
SUB = 4
MESH = pl.DeviceIdType.MESH
F32, BF16 = jnp.float32, jnp.bfloat16


def kernel(
    cell_ref, row_ref, col_ref, count_ref, tok_ref, ct_ref, blk_ref,
    y_ref, dx_ref, bg_ref,
    xall, ctall, ctt, wd, dxb, dxl, dxz, wb, wz,
    xs, xr, cs, cr, dxs, dxr, dzs, dzr, ws, wr, wzs, wzr, gzs, gzr, gxs, gxr, gfs, gfr, gcs, gcr,
):
    d, f = lax.axis_index("dp"), lax.axis_index("fsdp")
    zh, x, c = lax.div(d, 8), lax.rem(lax.div(d, 2), 4), lax.rem(d, 2)
    y, zl = lax.div(f, 2), lax.rem(f, 2)

    def at(dzh=0, dx=0, dc=0, dy=0, dzl=0):
        nzh, nx = lax.rem(zh + dzh + NZH, NZH), lax.rem(x + dx + NX, NX)
        nc, ny, nzl = lax.rem(c + dc, 2), lax.rem(y + dy + NY, NY), lax.rem(zl + dzl, 2)
        return ((nzh * 4 + nx) * 2 + nc, ny * 2 + nzl)

    yp, ym, zp, xp, xm = at(dy=1), at(dy=-1), at(dzl=1), at(dx=1), at(dx=-1)
    core = at(dc=1)
    zhs = [None, at(dzh=1), at(dzh=2), at(dzh=3)]

    barrier = pltpu.get_barrier_semaphore()
    for peer in (yp, ym, zp, xp, xm, core, *zhs[1:]):
        pl.semaphore_signal(barrier, inc=1, device_id=peer, device_id_type=MESH)

    def remote(src, dst, ss, rs, dev):
        return pltpu.make_async_remote_copy(
            src_ref=src, dst_ref=dst, send_sem=ss, recv_sem=rs, device_id=dev, device_id_type=MESH
        )

    base = c * TOK
    for b in range(4):
        xall[4 * f + b, pl.ds(base, TOK), :] = tok_ref[:, b * BLK : (b + 1) * BLK]
    ctall[pl.ds(base, TOK), :] = ct_ref[...]
    pl.semaphore_wait(barrier, 9)

    names = {}
    sent = []

    def src_f(dy, dzl):
        return lax.rem(y + dy + NY, NY) * 2 + lax.rem(zl + dzl, 2)

    def xpart(dy, dzl, r0, n):
        return xall.at[pl.ds(4 * src_f(dy, dzl), 4), pl.ds(base + r0, n), :]

    def send(name, dy, dzl, r0, n, dev):
        k = names.setdefault(name, len(names))
        part = xpart(dy, dzl, r0, n)
        copy = remote(part, part, xs.at[k], xr.at[k], dev)
        copy.start()
        sent.append(copy)

    def recv(name, dy, dzl, r0, n):
        k = names[name]
        part = xpart(dy, dzl, r0, n)
        remote(part, part, xs.at[k], xr.at[k], core).wait_recv()

    crossed = []

    def cross(dy, dzl):
        k = len(crossed)
        part = xall.at[pl.ds(4 * src_f(dy, dzl), 4), pl.ds(base, TOK), :]
        copy = remote(part, part, cs.at[k], cr.at[k], core)
        copy.start()
        sent.append(copy)
        crossed.append((dy, dzl))

    H = TOK // 2
    send("Z0", 0, 0, H, H, zp)
    send("P0", 0, 0, 0, TOK, yp)
    send("M0", 0, 0, 0, TOK, ym)
    ctcopy = remote(ctall.at[pl.ds(base, TOK)], ctall.at[pl.ds(base, TOK)], cs.at[16], cr.at[16], core)
    ctcopy.start()
    sent.append(ctcopy)
    cross(0, 0)
    send("ZA", 0, 0, 0, H, zp)

    def build(r, carry):
        for j in range(2):
            m = cell_ref[2 * r + j]
            b = blk_ref[jnp.maximum(m, 0)]
            b = jnp.where(m >= 0, b, jnp.zeros_like(b))
            wd[pl.ds(pl.multiple_of(r * BLK, BLK), BLK), j * BLK : (j + 1) * BLK] = b
        return carry

    lax.fori_loop(0, 64, build, 0)

    recv("Z0", 0, 1, H, H)
    send("OP0", 0, 1, H, H, yp)
    send("OM0", 0, 1, H, H, ym)
    for i in (1, 2, 3):
        last = i == 3
        recv(f"P{i - 1}", -i, 0, 0, TOK)
        send(f"P{i}", -i, 0, 0, H if last else TOK, yp)
        recv(f"M{i - 1}", i, 0, 0, TOK)
        send(f"M{i}", i, 0, H if last else 0, H if last else TOK, ym)
        send(f"ZP{i}", -i, 0, 0, H, zp)
        send(f"ZM{i}", i, 0, 0, H, zp)
        cross(-i, 0)
        cross(i, 0)
        recv(f"OP{i - 1}", -i, 1, H, H)
        send(f"OP{i}", -i, 1, H, H // 2 if last else H, yp)
        recv(f"OM{i - 1}", i, 1, H, H)
        send(f"OM{i}", i, 1, H + H // 2 if last else H, H // 2 if last else H, ym)
        if i == 1:
            recv("ZA", 0, 1, 0, H)
            cross(0, 1)
        else:
            recv(f"ZP{i - 1}", -(i - 1), 1, 0, H)
            recv(f"ZM{i - 1}", i - 1, 1, 0, H)
            cross(-(i - 1), 1)
            cross(i - 1, 1)

    def dx_target(way, s):
        return lax.rem(y - 1 - s + 2 * NY, NY) if way == 0 else lax.rem(y + 1 + s, NY)

    def dx_term(way, s):
        rows = pl.multiple_of(dx_target(way, s) * (2 * XF) + way * XF, XF)
        return lax.dot_general(
            ct_ref[...], wd[pl.ds(rows, XF), :], (((1,), (1,)), ((), ())), preferred_element_type=F32
        )

    R = TOK // SUB

    def dx_copy(way, s, j):
        rows = pl.ds(pl.multiple_of(j * R, R), R)
        return remote(
            dxb.at[way, s, rows], dxb.at[way, s + 1, rows],
            dxs.at[way, s, j], dxr.at[way, s + 1, j], yp if way == 0 else ym,
        )

    def dx_wait(way, s, j):
        rows = pl.ds(pl.multiple_of(j * R, R), R)
        remote(
            dxb.at[way, s, rows], dxb.at[way, s, rows], dxs.at[way, 0, j], dxr.at[way, s, j], core
        ).wait_recv()

    def dx_part(way, s, j):
        dx_wait(way, s, j)
        rows = pl.ds(pl.multiple_of(j * R, R), R)
        dxb[way, s, rows, :] = dxb[way, s, rows, :] + dxl[way, rows, :]

    def dx_terms(s):
        for way in (0, 1):
            dxl[way] = dx_term(way, s)

    for way in (0, 1):
        dxb[way, 0] = dx_term(way, 0)

    def first(j, carry):
        for way in (0, 1):
            dx_copy(way, 0, j).start()
        return carry

    lax.fori_loop(0, SUB, first, 0)

    recv("P3", -4, 0, 0, H)
    send("ZP4", -4, 0, 0, H, zp)
    recv("M3", -4, 0, H, H)
    cross(-4, 0)
    recv("ZP3", -3, 1, 0, H)
    recv("ZM3", 3, 1, 0, H)
    cross(-3, 1)
    cross(3, 1)
    recv("OP3", -4, 1, H, H // 2)
    recv("OM3", -4, 1, H + H // 2, H // 2)
    recv("ZP4", -4, 1, 0, H)
    cross(-4, 1)

    other = lax.rem(c + 1, 2) * TOK
    part = ctall.at[pl.ds(other, TOK)]
    remote(part, part, cs.at[16], cr.at[16], core).wait_recv()
    for j in range(2):
        ctt[j] = ctall[:, j * BLK : (j + 1) * BLK].astype(F32).T.astype(BF16)
    for k, (dy, dzl) in enumerate(crossed):
        part = xall.at[pl.ds(4 * src_f(dy, dzl), 4), pl.ds(other, TOK), :]
        remote(part, part, cs.at[k], cr.at[k], core).wait_recv()

    def dw_term(tx, tzh, way):
        s = c * 32 + tx * 8 + tzh * 2 + way
        return jnp.dot(ctt[col_ref[s]], xall[row_ref[s]], preferred_element_type=F32)

    def dw_target(way, s):
        return lax.rem(x - 1 - s + 2 * NX, NX) if way == 0 else lax.rem(x + 1 + s, NX)

    def dw_copy(way, s, j):
        return remote(
            wb.at[way, s, j], wb.at[way, s + 1, j], ws.at[way, s, j], wr.at[way, s + 1, j],
            xp if way == 0 else xm,
        )

    def dw_wait(way, s, j):
        remote(wb.at[way, s, j], wb.at[way, s, j], ws.at[way, 0, j], wr.at[way, s, j], core).wait_recv()

    def part_zh(j):
        return lax.rem(zh + 1 + j, NZH)

    def dw_first(j, carry):
        for way in (0, 1):
            wb[way, 0, j] = dw_term(dw_target(way, 0), part_zh(j), way)
            dw_copy(way, 0, j).start()
        return carry

    lax.fori_loop(0, 4, dw_first, 0)

    def y_step(k, acc):
        rows = pl.ds(pl.multiple_of(k * 2 * BLK, 2 * BLK), 2 * BLK)
        xb = jnp.concatenate([xall[2 * k + b, pl.ds(base, TOK), :] for b in range(2)], axis=1)
        return acc + jnp.dot(xb, wd[rows, :], preferred_element_type=F32)

    y_ref[...] = lax.fori_loop(0, 32, y_step, jnp.zeros((TOK, CF), F32)).astype(BF16)

    for s in (1, 2):
        dx_terms(s)

        def both(j, carry, s=s):
            for way in (0, 1):
                term = dw_term(dw_target(way, s), part_zh(j), way)
                dw_wait(way, s, j)
                wb[way, s, j] = wb[way, s, j] + term
                dw_copy(way, s, j).start()
            for way in (0, 1):
                dx_part(way, s, j)
                dx_copy(way, s, j).start()
            return carry

        lax.fori_loop(0, SUB, both, 0)

    dx_terms(3)

    def wz_copy(way, j):
        return remote(wb.at[way, 3, j], wz.at[way, j], wzs.at[way, j], wzr.at[way, j], zhs[j + 1])

    for j in range(4):
        for way in (0, 1):
            term = dw_term(x, part_zh(j), way)
            dw_wait(way, 3, j)
            wb[way, 3, j] = wb[way, 3, j] + term
            if j < 3:
                wz_copy(way, j).start()
        for way in (0, 1):
            dx_part(way, 3, j)
            dx_copy(way, 3, j).start()

    def dx_round(s):
        dx_terms(s)

        def step(j, carry):
            for way in (0, 1):
                dx_part(way, s, j)
                dx_copy(way, s, j).start()
            return carry

        lax.fori_loop(0, SUB, step, 0)

    dx_round(4)

    mine = c * 32 + x * 8 + zh * 2
    for way in (0, 1):
        total = wb[way, 3, 3]
        for j in range(3):
            remote(wz.at[way, j], wz.at[way, j], wzs.at[way, j], wzr.at[way, j], core).wait_recv()
            total = total + wz[way, j]
        total = jnp.where(mine + way < count_ref[0], total.T, jnp.zeros((BLK, BLK), F32))
        bg_ref[mine + way] = total.astype(BF16)

    def slots(dx, dzh, n=2):
        return bg_ref.at[pl.ds(c * 32 + lax.rem(x + dx + NX, NX) * 8 + lax.rem(zh + dzh + NZH, NZH) * 2, n)]

    def gx_copy(way, k):
        part = slots(0, -k)
        return remote(part, part, gxs.at[way, k], gxr.at[way, k], xp if way == 0 else xm)

    for k in (1, 2, 3):
        part = slots(0, 0)
        copy = remote(part, part, gzs.at[k], gzr.at[k], zhs[k])
        copy.start()
        sent.append(copy)
    for k in range(4):
        if k:
            part = slots(0, -k)
            remote(part, part, gzs.at[k], gzr.at[k], core).wait_recv()
        for way in (0, 1):
            copy = gx_copy(way, k)
            copy.start()
            sent.append(copy)

    def whole(c_, dx):
        return bg_ref.at[pl.ds(c_ * 32 + lax.rem(x + dx + NX, NX) * 8, 8)]

    def over(k, dx):
        part = whole(c, dx)
        copy = remote(part, part, gcs.at[k], gcr.at[k], core)
        copy.start()
        sent.append(copy)

    over(0, 0)
    dx_round(5)
    for k in range(4):
        for way, dx in ((0, -1), (1, 1)):
            part = slots(dx, -k)
            remote(part, part, gxs.at[way, k], gxr.at[way, k], core).wait_recv()
            if (k < 2) == (way == 0):
                copy = remote(part, part, gfs.at[k], gfr.at[k], xp if way == 0 else xm)
                copy.start()
                sent.append(copy)
    over(1, -1)
    over(2, 1)
    dx_round(6)
    for k in range(4):
        part = slots(2, -k)
        remote(part, part, gfs.at[k], gfr.at[k], core).wait_recv()
    over(3, 2)

    dx_terms(7)

    def z_copy(j):
        rows = pl.ds(pl.multiple_of(j * R, R), R)
        return remote(dxb.at[1 - zl, 7, rows], dxz.at[rows], dzs.at[j], dzr.at[j], zp)

    for j in range(SUB):
        for way in (0, 1):
            dx_part(way, 7, j)
        z_copy(j).start()
    for j in range(SUB):
        rows = pl.ds(j * R, R)
        remote(dxz.at[rows], dxz.at[rows], dzs.at[j], dzr.at[j], core).wait_recv()
        dx_ref[rows, :] = (dxb[zl, 7, rows, :] + dxz[rows, :]).astype(BF16)

    for k, dx in enumerate((0, -1, 1, 2)):
        part = whole(1 - c, dx)
        remote(part, part, gcs.at[k], gcr.at[k], core).wait_recv()

    for copy in sent:
        copy.wait_send()
    for j in range(SUB):
        z_copy(j).wait_send()
    for way in (0, 1):
        for j in range(3):
            wz_copy(way, j).wait_send()

        def left(n, carry, way=way):
            dx_copy(way, lax.div(n, SUB), lax.rem(n, SUB)).wait_send()
            return carry

        lax.fori_loop(0, 7 * SUB, left, 0)

        def gone(n, carry, way=way):
            dw_copy(way, lax.div(n, 4), lax.rem(n, 4)).wait_send()
            return carry

        lax.fori_loop(0, 3 * 4, gone, 0)


def per_device(tokens, cotangent, blocks, slot_block, shard_count):
    row, col = slot_block // 32, slot_block % 2
    cell = row * 2 + col
    place = jnp.arange(64, dtype=jnp.int32)
    here = (cell[:, None] == jnp.arange(128, dtype=jnp.int32)[None, :]) & (place < shard_count[0])[:, None]
    cell_slot = jnp.max(jnp.where(here, place[:, None], -1), axis=0)
    smem, vmem = pl.BlockSpec(memory_space=pltpu.SMEM), pl.BlockSpec(memory_space=pltpu.VMEM)
    dma = pltpu.SemaphoreType.DMA
    return pl.pallas_call(
        kernel,
        out_shape=(
            jax.ShapeDtypeStruct((TOK, CF), BF16),
            jax.ShapeDtypeStruct((TOK, XF), BF16),
            jax.ShapeDtypeStruct((64, BLK, BLK), BF16),
        ),
        in_specs=[smem] * 4 + [vmem] * 3,
        out_specs=(vmem,) * 3,
        scratch_shapes=[
            pltpu.VMEM((64, 2 * TOK, BLK), BF16),
            pltpu.VMEM((2 * TOK, CF), BF16),
            pltpu.VMEM((2, BLK, 2 * TOK), BF16),
            pltpu.VMEM((64 * BLK, CF), BF16),
            pltpu.VMEM((2, 8, TOK, XF), F32),
            pltpu.VMEM((2, TOK, XF), F32),
            pltpu.VMEM((TOK, XF), F32),
            pltpu.VMEM((2, 4, 4, BLK, BLK), F32),
            pltpu.VMEM((2, 3, BLK, BLK), F32),
            dma((32,)), dma((32,)), dma((17,)), dma((17,)),
            dma((2, 8, SUB)), dma((2, 8, SUB)), dma((SUB,)), dma((SUB,)),
            dma((2, 4, 4)), dma((2, 4, 4)), dma((2, 3)), dma((2, 3)),
            dma((4,)), dma((4,)), dma((2, 4)), dma((2, 4)), dma((4,)), dma((4,)), dma((4,)), dma((4,)),
        ],
        compiler_params=pltpu.CompilerParams(
            collective_id=0, has_side_effects=True, vmem_limit_bytes=48 << 20
        ),
    )(cell_slot, row, col, shard_count, tokens, cotangent, blocks)


def solution(mesh):
    return jax.shard_map(
        per_device,
        mesh=mesh,
        in_specs=(P("dp", "fsdp"), P("dp", "fsdp"), P("fsdp", None, None), P("fsdp"), P("fsdp")),
        out_specs=(P("dp", "fsdp"), P("dp", "fsdp"), P("fsdp", None, None)),
        check_vma=False,
    )
```

```python
import functools

import jax
import jax.numpy as jnp
from jax import lax
from jax.experimental import pallas as pl
from jax.experimental.pallas import tpu as pltpu
from jax.sharding import PartitionSpec as P

BLK = 128
NY, NZL, NX, NZH = 8, 2, 4, 4
TOK = 128
XF = 512
CF = 256
SUB = 4
MESH = pl.DeviceIdType.MESH
F32, BF16 = jnp.float32, jnp.bfloat16


CODE = 72
STEPS = 32760.0


def encode(ref, value):
    tiles = value.reshape(16, 8, BLK)
    top = jnp.max(jnp.abs(tiles), axis=0)
    power = jnp.ceil(jnp.log2(jnp.maximum(top, 1e-33)) * 8.0)
    code = jnp.round(tiles * (jnp.exp2(power * -0.125) * STEPS)[None]).astype(jnp.int32)
    pairs = lax.shift_left(code[:8], jnp.full((8, 8, BLK), 16, jnp.int32)) | (code[8:] & 0xFFFF)
    ref[0:64, :] = pairs.reshape(64, BLK)
    ref[64:CODE, :] = power.astype(jnp.int32)


def decode(ref):
    pairs = ref[0:64, :].reshape(8, 8, BLK)
    scale = jnp.exp2(ref[64:CODE, :].astype(F32) * 0.125) * (1.0 / STEPS)
    by = jnp.full((8, 8, BLK), 16, jnp.int32)
    high = lax.shift_right_arithmetic(pairs, by)
    low = lax.shift_right_arithmetic(lax.shift_left(pairs, by), by)
    tiles = jnp.concatenate([high, low], axis=0).astype(F32) * scale[None]
    return tiles.reshape(BLK, BLK)


def kernel(
    cell_ref, row_ref, col_ref, count_ref, tok_hbm, ct_hbm, blk_hbm,
    y_ref, dx_ref, bg_ref,
    xall, ctall, ctt, blk_ref, wd, yacc, dxb, dxf, dxz, wb, wf, wz,
    ls, xs, xr, cs, cr, dxs, dxr, dzs, dzr, ws, wr, wzs, wzr, gzs, gzr, gxs, gxr, gfs, gfr, gcs, gcr,
):
    d, f = lax.axis_index("dp"), lax.axis_index("fsdp")
    zh, x, c = lax.div(d, 8), lax.rem(lax.div(d, 2), 4), lax.rem(d, 2)
    y, zl = lax.div(f, 2), lax.rem(f, 2)

    def at(dzh=0, dx=0, dc=0, dy=0, dzl=0):
        nzh, nx = lax.rem(zh + dzh + NZH, NZH), lax.rem(x + dx + NX, NX)
        nc, ny, nzl = lax.rem(c + dc, 2), lax.rem(y + dy + NY, NY), lax.rem(zl + dzl, 2)
        return ((nzh * 4 + nx) * 2 + nc, ny * 2 + nzl)

    yp, ym, zp, xp, xm = at(dy=1), at(dy=-1), at(dzl=1), at(dx=1), at(dx=-1)
    core = at(dc=1)
    zhs = [None, at(dzh=1), at(dzh=2), at(dzh=3)]
    base = c * TOK

    barrier = pltpu.get_barrier_semaphore()
    for peer in (yp, ym, zp, xp, xm, core, *zhs[1:]):
        pl.semaphore_signal(barrier, inc=1, device_id=peer, device_id_type=MESH)

    loads = [
        pltpu.make_async_copy(tok_hbm.at[:, pl.ds(b * BLK, BLK)], xall.at[4 * f + b, pl.ds(base, TOK)], ls.at[b])
        for b in range(4)
    ]
    loads.append(pltpu.make_async_copy(ct_hbm, ctall.at[pl.ds(base, TOK)], ls.at[4]))
    loads.append(pltpu.make_async_copy(blk_hbm, blk_ref, ls.at[5]))
    for load in loads:
        load.start()

    def remote(src, dst, ss, rs, dev):
        return pltpu.make_async_remote_copy(
            src_ref=src, dst_ref=dst, send_sem=ss, recv_sem=rs, device_id=dev, device_id_type=MESH
        )

    names = {}
    sent = []

    def src_f(dy, dzl):
        return lax.rem(y + dy + NY, NY) * 2 + lax.rem(zl + dzl, 2)

    def xpart(dy, dzl, r0, n, start=base):
        return xall.at[pl.ds(4 * src_f(dy, dzl), 4), pl.ds(start + r0, n), :]

    def send(name, dy, dzl, r0, n, dev):
        k = names.setdefault(name, len(names))
        part = xpart(dy, dzl, r0, n)
        copy = remote(part, part, xs.at[k], xr.at[k], dev)
        copy.start()
        sent.append(copy)

    def recv(name, dy, dzl, r0, n):
        k = names[name]
        part = xpart(dy, dzl, r0, n)
        remote(part, part, xs.at[k], xr.at[k], core).wait_recv()

    crossed = []

    def cross(dy, dzl):
        k = len(crossed)
        part = xpart(dy, dzl, 0, TOK)
        copy = remote(part, part, cs.at[k], cr.at[k], core)
        copy.start()
        sent.append(copy)
        crossed.append((dy, dzl))

    H = TOK // 2
    Q = TOK // 4
    for load in loads[:5]:
        load.wait()
    pl.semaphore_wait(barrier, 9)
    send("Z0", 0, 0, H, H, zp)
    send("PA0", 0, 0, 0, H, yp)
    send("MA0", 0, 0, 0, H, ym)
    send("PB0", 0, 0, H, H, yp)
    send("MB0", 0, 0, H, H, ym)
    send("ZA", 0, 0, 0, H, zp)
    ctpart = ctall.at[pl.ds(base, TOK)]
    ctcopy = remote(ctpart, ctpart, cs.at[16], cr.at[16], core)
    ctcopy.start()
    sent.append(ctcopy)
    cross(0, 0)
    loads[5].wait()

    def build(r, carry):
        for j in range(2):
            m = cell_ref[2 * r + j]
            b = blk_ref[jnp.maximum(m, 0)]
            b = jnp.where(m >= 0, b, jnp.zeros_like(b))
            wd[pl.ds(pl.multiple_of(r * BLK, BLK), BLK), j * BLK : (j + 1) * BLK] = b
        return carry

    recv("Z0", 0, 1, H, H)
    send("OP0", 0, 1, H, H, yp)
    send("OM0", 0, 1, H, H, ym)
    for i in (1, 2, 3):
        last = i == 3
        recv(f"PA{i - 1}", -i, 0, 0, H)
        send(f"PA{i}", -i, 0, 0, H, yp)
        send(f"ZP{i}", -i, 0, 0, H, zp)
        recv(f"MA{i - 1}", i, 0, 0, H)
        if not last:
            send(f"MA{i}", i, 0, 0, H, ym)
        send(f"ZM{i}", i, 0, 0, H, zp)
        recv(f"PB{i - 1}", -i, 0, H, H)
        if not last:
            send(f"PB{i}", -i, 0, H, H, yp)
        recv(f"MB{i - 1}", i, 0, H, H)
        send(f"MB{i}", i, 0, H, H, ym)
        cross(-i, 0)
        cross(i, 0)
        recv(f"OP{i - 1}", -i, 1, H, H)
        send(f"OP{i}", -i, 1, H, Q if last else H, yp)
        recv(f"OM{i - 1}", i, 1, H, H)
        send(f"OM{i}", i, 1, H + Q if last else H, Q if last else H, ym)
        lax.fori_loop((i - 1) * 24, min(i * 24, 64), build, 0)
        if i == 1:
            recv("ZA", 0, 1, 0, H)
            cross(0, 1)
        else:
            recv(f"ZP{i - 1}", -(i - 1), 1, 0, H)
            recv(f"ZM{i - 1}", i - 1, 1, 0, H)
            cross(-(i - 1), 1)
            cross(i - 1, 1)

    def dx_target(way, s):
        return lax.rem(y - 1 - s + 2 * NY, NY) if way == 0 else lax.rem(y + 1 + s, NY)

    def dx_term(way, s, j):
        rows = pl.multiple_of(dx_target(way, s) * (2 * XF) + way * XF + j * BLK, BLK)
        return lax.dot_general(
            ctall[pl.ds(base, TOK), :], wd[pl.ds(rows, BLK), :], (((1,), (1,)), ((), ())), preferred_element_type=F32
        )

    def dx_copy(way, s, j):
        return remote(
            dxb.at[way, s, j], dxb.at[way, s + 1, j], dxs.at[way, s, j], dxr.at[way, s + 1, j],
            yp if way == 0 else ym,
        )

    def dx_part(way, s, j):
        term = dx_term(way, s, j)
        part = dxb.at[way, s, j]
        remote(part, part, dxs.at[way, 0, j], dxr.at[way, s, j], core).wait_recv()
        return term + decode(part)

    def dx_first(j, carry):
        for way in (0, 1):
            encode(dxb.at[way, 0, j], dx_term(way, 0, j))
            dx_copy(way, 0, j).start()
        return carry

    def dx_round(s):
        def step(j, carry):
            for way in (0, 1):
                encode(dxb.at[way, s, j], dx_part(way, s, j))
                dx_copy(way, s, j).start()
            return carry

        lax.fori_loop(0, SUB, step, 0)

    lax.fori_loop(0, SUB, dx_first, 0)

    recv("PA3", -4, 0, 0, H)
    send("ZP4", -4, 0, 0, H, zp)
    recv("MB3", -4, 0, H, H)
    cross(-4, 0)
    recv("ZP3", -3, 1, 0, H)
    recv("ZM3", 3, 1, 0, H)
    cross(-3, 1)
    cross(3, 1)
    recv("OP3", -4, 1, H, Q)
    recv("OM3", -4, 1, H + Q, Q)
    recv("ZP4", -4, 1, 0, H)
    cross(-4, 1)

    other = lax.rem(c + 1, 2) * TOK
    part = ctall.at[pl.ds(other, TOK)]
    remote(part, part, cs.at[16], cr.at[16], core).wait_recv()
    for j in range(2):
        ctt[j] = ctall[:, j * BLK : (j + 1) * BLK].astype(F32).T.astype(BF16)
    for k, (dy, dzl) in enumerate(crossed):
        part = xpart(dy, dzl, 0, TOK, other)
        remote(part, part, cs.at[k], cr.at[k], core).wait_recv()

    def dw_term(tx, tzh, way):
        s = c * 32 + tx * 8 + tzh * 2 + way
        return jnp.dot(ctt[col_ref[s]], xall[row_ref[s]], preferred_element_type=F32)

    def dw_target(way, s):
        return lax.rem(x - 1 - s + 2 * NX, NX) if way == 0 else lax.rem(x + 1 + s, NX)

    def dw_copy(way, s, j):
        return remote(
            wb.at[way, s, j], wb.at[way, s + 1, j], ws.at[way, s, j], wr.at[way, s + 1, j],
            xp if way == 0 else xm,
        )

    def part_zh(j):
        return lax.rem(zh + 1 + j, NZH)

    def dw_part(way, s, j):
        term = dw_term(dw_target(way, s), part_zh(j), way)
        part = wb.at[way, s, j]
        remote(part, part, ws.at[way, 0, j], wr.at[way, s, j], core).wait_recv()
        return term + decode(part)

    def dw_first(j, carry):
        for way in (0, 1):
            encode(wb.at[way, 0, j], dw_term(dw_target(way, 0), part_zh(j), way))
            dw_copy(way, 0, j).start()
        return carry

    def dw_round(s):
        def step(j, carry):
            for way in (0, 1):
                encode(wb.at[way, s, j], dw_part(way, s, j))
                dw_copy(way, s, j).start()
            return carry

        lax.fori_loop(0, 4, step, 0)

    def y_part(k):
        xb = jnp.concatenate([xall[8 * k + b, pl.ds(base, TOK), :] for b in range(8)], axis=1)
        rows = pl.ds(pl.multiple_of(k * 8 * BLK, 8 * BLK), 8 * BLK)
        term = jnp.dot(xb, wd[rows, :], preferred_element_type=F32)
        yacc[...] = term if k == 0 else yacc[...] + term

    lax.fori_loop(0, 4, dw_first, 0)
    dx_round(1)
    y_part(0)
    dw_round(1)
    y_part(1)
    dx_round(2)
    y_part(2)
    dw_round(2)
    y_part(3)
    dx_round(3)
    y_part(4)

    def wz_copy(way, j):
        return remote(wb.at[way, 0, j], wz.at[way, j], wzs.at[way, j], wzr.at[way, j], zhs[j + 1])

    for way in (0, 1):
        for j in range(3):
            dw_copy(way, 0, j).wait_send()
    for j in range(4):
        for way in (0, 1):
            total = dw_part(way, 3, j)
            if j < 3:
                encode(wb.at[way, 0, j], total)
                wz_copy(way, j).start()
            else:
                wf[way] = total
    dx_round(4)
    y_part(5)
    dx_round(5)

    mine = c * 32 + x * 8 + zh * 2
    for way in (0, 1):
        total = wf[way]
        for j in range(3):
            part = wz.at[way, j]
            remote(part, part, wzs.at[way, j], wzr.at[way, j], core).wait_recv()
            total = total + decode(part)
        total = jnp.where(mine + way < count_ref[0], total.T, jnp.zeros((BLK, BLK), F32))
        bg_ref[mine + way] = total.astype(BF16)

    def slots(dx, dzh, n=2):
        return bg_ref.at[pl.ds(c * 32 + lax.rem(x + dx + NX, NX) * 8 + lax.rem(zh + dzh + NZH, NZH) * 2, n)]

    def gx_send(k):
        part = slots(0, -k)
        for way in (0, 1):
            copy = remote(part, part, gxs.at[way, k], gxr.at[way, k], xp if way == 0 else xm)
            copy.start()
            sent.append(copy)

    def gx_pass(k):
        for way, dx in ((0, -1), (1, 1)):
            part = slots(dx, -k)
            remote(part, part, gxs.at[way, k], gxr.at[way, k], core).wait_recv()
            if (k < 2) == (way == 0):
                copy = remote(part, part, gfs.at[k], gfr.at[k], xp if way == 0 else xm)
                copy.start()
                sent.append(copy)

    def whole(c_, dx):
        return bg_ref.at[pl.ds(c_ * 32 + lax.rem(x + dx + NX, NX) * 8, 8)]

    def over(k, dx):
        part = whole(c, dx)
        copy = remote(part, part, gcs.at[k], gcr.at[k], core)
        copy.start()
        sent.append(copy)

    gx_send(0)
    for k in (1, 2, 3):
        part = slots(0, 0)
        copy = remote(part, part, gzs.at[k], gzr.at[k], zhs[k])
        copy.start()
        sent.append(copy)
    dx_round(6)
    for k in (1, 3, 2):
        part = slots(0, -k)
        remote(part, part, gzs.at[k], gzr.at[k], core).wait_recv()
        gx_send(k)
    over(0, 0)
    gx_pass(0)

    def z_copy(j):
        return remote(dxb.at[1 - zl, 0, j], dxz.at[j], dzs.at[j], dzr.at[j], zp)

    for way in (0, 1):
        for j in range(SUB):
            dx_copy(way, 0, j).wait_send()
    for j in range(SUB):
        for way in (0, 1):
            dxf[way, j] = dx_part(way, 7, j)
        encode(dxb.at[1 - zl, 0, j], dxf[1 - zl, j])
        z_copy(j).start()
    y_part(6)
    gx_pass(1)
    y_part(7)
    y_ref[...] = yacc[...].astype(BF16)
    gx_pass(3)
    gx_pass(2)
    over(1, -1)
    over(2, 1)
    for j in range(SUB):
        part = dxz.at[j]
        remote(part, part, dzs.at[j], dzr.at[j], core).wait_recv()
        dx_ref[:, j * BLK : (j + 1) * BLK] = (dxf[zl, j] + decode(part)).astype(BF16)
    for k in range(4):
        part = slots(2, -k)
        remote(part, part, gfs.at[k], gfr.at[k], core).wait_recv()
    over(3, 2)
    for k, dx in enumerate((0, -1, 1, 2)):
        part = whole(1 - c, dx)
        remote(part, part, gcs.at[k], gcr.at[k], core).wait_recv()

    for copy in sent:
        copy.wait_send()
    for j in range(SUB):
        z_copy(j).wait_send()
    for way in (0, 1):
        for j in range(3):
            wz_copy(way, j).wait_send()
        dw_copy(way, 0, 3).wait_send()

        def left(n, carry, way=way):
            dx_copy(way, lax.div(n, SUB), lax.rem(n, SUB)).wait_send()
            return carry

        lax.fori_loop(SUB, 7 * SUB, left, 0)

        def gone(n, carry, way=way):
            dw_copy(way, lax.div(n, 4), lax.rem(n, 4)).wait_send()
            return carry

        lax.fori_loop(4, 3 * 4, gone, 0)


def per_device(tokens, cotangent, blocks, slot_block, shard_count):
    row, col = slot_block // 32, slot_block % 2
    cell = row * 2 + col
    place = jnp.arange(64, dtype=jnp.int32)
    here = (cell[:, None] == jnp.arange(128, dtype=jnp.int32)[None, :]) & (place < shard_count[0])[:, None]
    cell_slot = jnp.max(jnp.where(here, place[:, None], -1), axis=0)
    smem, vmem, hbm = (pl.BlockSpec(memory_space=m) for m in (pltpu.SMEM, pltpu.VMEM, pltpu.HBM))
    dma = pltpu.SemaphoreType.DMA
    return pl.pallas_call(
        kernel,
        out_shape=(
            jax.ShapeDtypeStruct((TOK, CF), BF16),
            jax.ShapeDtypeStruct((TOK, XF), BF16),
            jax.ShapeDtypeStruct((64, BLK, BLK), BF16),
        ),
        in_specs=[smem] * 4 + [hbm] * 3,
        out_specs=(vmem,) * 3,
        scratch_shapes=[
            pltpu.VMEM((64, 2 * TOK, BLK), BF16),
            pltpu.VMEM((2 * TOK, CF), BF16),
            pltpu.VMEM((2, BLK, 2 * TOK), BF16),
            pltpu.VMEM((64, BLK, BLK), BF16),
            pltpu.VMEM((64 * BLK, CF), BF16),
            pltpu.VMEM((TOK, CF), F32),
            pltpu.VMEM((2, 8, SUB, CODE, BLK), jnp.int32),
            pltpu.VMEM((2, SUB, BLK, BLK), F32),
            pltpu.VMEM((SUB, CODE, BLK), jnp.int32),
            pltpu.VMEM((2, 4, 4, CODE, BLK), jnp.int32),
            pltpu.VMEM((2, BLK, BLK), F32),
            pltpu.VMEM((2, 3, CODE, BLK), jnp.int32),
            dma((6,)), dma((40,)), dma((40,)), dma((17,)), dma((17,)),
            dma((2, 8, SUB)), dma((2, 8, SUB)), dma((SUB,)), dma((SUB,)),
            dma((2, 4, 4)), dma((2, 4, 4)), dma((2, 3)), dma((2, 3)),
            dma((4,)), dma((4,)), dma((2, 4)), dma((2, 4)), dma((4,)), dma((4,)), dma((4,)), dma((4,)),
        ],
        compiler_params=pltpu.CompilerParams(
            collective_id=0, has_side_effects=True, vmem_limit_bytes=48 << 20
        ),
    )(cell_slot, row, col, shard_count, tokens, cotangent, blocks)


def solution(mesh):
    return jax.shard_map(
        per_device,
        mesh=mesh,
        in_specs=(P("dp", "fsdp"), P("dp", "fsdp"), P("fsdp", None, None), P("fsdp"), P("fsdp")),
        out_specs=(P("dp", "fsdp"), P("dp", "fsdp"), P("fsdp", None, None)),
        check_vma=False,
    )
```

```python
import functools

import jax
import jax.numpy as jnp
from jax import lax
from jax.experimental import pallas as pl
from jax.experimental.pallas import tpu as pltpu
from jax.sharding import PartitionSpec as P

BLK = 128
NY, NZL, NX, NZH = 8, 2, 4, 4
TOK = 128
XF = 512
CF = 256
SUB = 4
MESH = pl.DeviceIdType.MESH
F32, BF16 = jnp.float32, jnp.bfloat16


CODE = 72
STEPS = 32760.0


def encode(ref, value):
    tiles = value.reshape(16, 8, BLK)
    top = jnp.max(jnp.abs(tiles), axis=0)
    power = jnp.ceil(jnp.log2(jnp.maximum(top, 1e-33)) * 8.0)
    code = jnp.round(tiles * (jnp.exp2(power * -0.125) * STEPS)[None]).astype(jnp.int32)
    pairs = lax.shift_left(code[:8], jnp.full((8, 8, BLK), 16, jnp.int32)) | (code[8:] & 0xFFFF)
    ref[0:64, :] = pairs.reshape(64, BLK)
    ref[64:CODE, :] = power.astype(jnp.int32)


def decode(ref):
    pairs = ref[0:64, :].reshape(8, 8, BLK)
    scale = jnp.exp2(ref[64:CODE, :].astype(F32) * 0.125) * (1.0 / STEPS)
    by = jnp.full((8, 8, BLK), 16, jnp.int32)
    high = lax.shift_right_arithmetic(pairs, by)
    low = lax.shift_right_arithmetic(lax.shift_left(pairs, by), by)
    tiles = jnp.concatenate([high, low], axis=0).astype(F32) * scale[None]
    return tiles.reshape(BLK, BLK)


def kernel(
    table_ref, tok_hbm, ct_hbm, blk_hbm,
    y_ref, dx_ref, bg_ref,
    xall, ctall, ctt, blk_ref, wd, yacc, dxt, dxb, dxf, dxz, wsb, wrb, wf, zsb, zrb, bgv, youtv, dxv,
    ls, xs, xr, cs, cr, dxs, dxr, dzs, dzr, ws, wr, wzs, wzr, gzs, gzr, gxs, gxr, gfs, gfr, gcs, gcr, os,
):
    d, f = lax.axis_index("dp"), lax.axis_index("fsdp")
    zh, x, c = lax.div(d, 8), lax.rem(lax.div(d, 2), 4), lax.rem(d, 2)
    y, zl = lax.div(f, 2), lax.rem(f, 2)

    def at(dzh=0, dx=0, dc=0, dy=0, dzl=0):
        nzh, nx = lax.rem(zh + dzh + NZH, NZH), lax.rem(x + dx + NX, NX)
        nc, ny, nzl = lax.rem(c + dc, 2), lax.rem(y + dy + NY, NY), lax.rem(zl + dzl, 2)
        return ((nzh * 4 + nx) * 2 + nc, ny * 2 + nzl)

    yp, ym, zp, xp, xm = at(dy=1), at(dy=-1), at(dzl=1), at(dx=1), at(dx=-1)
    core = at(dc=1)
    zhs = [None, at(dzh=1), at(dzh=2), at(dzh=3)]
    xs_to = [xp, at(dx=2), xm]
    base = c * TOK

    barrier = pltpu.get_barrier_semaphore()
    for peer in (yp, ym, zp, *xs_to, core, *zhs[1:]):
        pl.semaphore_signal(barrier, inc=1, device_id=peer, device_id_type=MESH)

    loads = [
        pltpu.make_async_copy(tok_hbm.at[:, pl.ds(b * BLK, BLK)], xall.at[4 * f + b, pl.ds(base, TOK)], ls.at[b])
        for b in range(4)
    ]
    loads.append(pltpu.make_async_copy(ct_hbm, ctall.at[pl.ds(base, TOK)], ls.at[4]))
    loads.append(pltpu.make_async_copy(blk_hbm, blk_ref, ls.at[5]))
    for load in loads:
        load.start()

    def remote(src, dst, ss, rs, dev):
        return pltpu.make_async_remote_copy(
            src_ref=src, dst_ref=dst, send_sem=ss, recv_sem=rs, device_id=dev, device_id_type=MESH
        )

    names = {}
    sent = []

    def src_f(dy, dzl):
        return lax.rem(y + dy + NY, NY) * 2 + lax.rem(zl + dzl, 2)

    def xpart(dy, dzl, r0, n, start=base):
        return xall.at[pl.ds(4 * src_f(dy, dzl), 4), pl.ds(start + r0, n), :]

    def send(name, dy, dzl, r0, n, dev):
        k = names.setdefault(name, len(names))
        part = xpart(dy, dzl, r0, n)
        copy = remote(part, part, xs.at[k], xr.at[k], dev)
        copy.start()
        sent.append(copy)

    def recv(name, dy, dzl, r0, n):
        k = names[name]
        part = xpart(dy, dzl, r0, n)
        remote(part, part, xs.at[k], xr.at[k], core).wait_recv()

    crossed = []

    def cross(dy, dzl):
        k = len(crossed)
        part = xpart(dy, dzl, 0, TOK)
        copy = remote(part, part, cs.at[k], cr.at[k], core)
        copy.start()
        sent.append(copy)
        crossed.append((dy, dzl))

    H = TOK // 2
    Q = TOK // 4
    for load in loads[:5]:
        load.wait()
    pl.semaphore_wait(barrier, 10)
    send("Z0", 0, 0, H, H, zp)
    send("PA0", 0, 0, 0, H, yp)
    send("MA0", 0, 0, 0, H, ym)
    send("PB0", 0, 0, H, H, yp)
    send("MB0", 0, 0, H, H, ym)
    send("ZA", 0, 0, 0, H, zp)
    ctpart = ctall.at[pl.ds(base, TOK)]
    ctcopy = remote(ctpart, ctpart, cs.at[16], cr.at[16], core)
    ctcopy.start()
    sent.append(ctcopy)
    cross(0, 0)
    loads[5].wait()

    def build(r, carry):
        for j in range(2):
            m = table_ref[2 * r + j]
            b = blk_ref[jnp.maximum(m, 0)]
            b = jnp.where(m >= 0, b, jnp.zeros_like(b))
            wd[pl.ds(pl.multiple_of(r * BLK, BLK), BLK), j * BLK : (j + 1) * BLK] = b
        return carry

    def dx_target(way, s):
        return lax.rem(y - 1 - s + 2 * NY, NY) if way == 0 else lax.rem(y + 1 + s, NY)

    def dx_terms(s):
        for way in (0, 1):
            rows = pl.multiple_of(dx_target(way, s) * (2 * XF) + way * XF, XF)
            terms = lax.dot_general(
                ctall[pl.ds(base, TOK), :], wd[pl.ds(rows, XF), :], (((1,), (1,)), ((), ())), preferred_element_type=F32
            )
            for j in range(SUB):
                dxt[way, s, j] = terms[:, j * BLK : (j + 1) * BLK]

    def dx_copy(way, s, j):
        return remote(
            dxb.at[way, s, j], dxb.at[way, s + 1, j], dxs.at[way, s, j], dxr.at[way, s + 1, j],
            yp if way == 0 else ym,
        )

    def dx_part(way, s, j):
        part = dxb.at[way, s, j]
        remote(part, part, dxs.at[way, 0, j], dxr.at[way, s, j], core).wait_recv()
        return dxt[way, s, j] + decode(part)

    def dx_first(j, carry):
        for way in (0, 1):
            encode(dxb.at[way, 0, j], dxt[way, 0, j])
            dx_copy(way, 0, j).start()
        return carry

    def dx_round(s):
        def step(j, carry):
            for way in (0, 1):
                encode(dxb.at[way, s, j], dx_part(way, s, j))
                dx_copy(way, s, j).start()
            return carry

        lax.fori_loop(0, SUB, step, 0)

    def y_part(dy, dzl, first=False):
        k = src_f(dy, dzl)
        xb = jnp.concatenate([xall[4 * k + b, pl.ds(base, TOK), :] for b in range(4)], axis=1)
        rows = pl.ds(pl.multiple_of(k * XF, XF), XF)
        term = jnp.dot(xb, wd[rows, :], preferred_element_type=F32)
        yacc[...] = term if first else yacc[...] + term

    lax.fori_loop(0, 64, build, 0)
    y_part(0, 0, True)
    recv("Z0", 0, 1, H, H)
    send("OP0", 0, 1, H, H, yp)
    send("OM0", 0, 1, H, H, ym)
    dx_terms(0)
    for i in (1, 2, 3):
        last = i == 3
        recv(f"PA{i - 1}", -i, 0, 0, H)
        send(f"PA{i}", -i, 0, 0, H, yp)
        send(f"ZP{i}", -i, 0, 0, H, zp)
        recv(f"MA{i - 1}", i, 0, 0, H)
        if not last:
            send(f"MA{i}", i, 0, 0, H, ym)
        send(f"ZM{i}", i, 0, 0, H, zp)
        recv(f"PB{i - 1}", -i, 0, H, H)
        if not last:
            send(f"PB{i}", -i, 0, H, H, yp)
        recv(f"MB{i - 1}", i, 0, H, H)
        send(f"MB{i}", i, 0, H, H, ym)
        cross(-i, 0)
        cross(i, 0)
        recv(f"OP{i - 1}", -i, 1, H, H)
        send(f"OP{i}", -i, 1, H, Q if last else H, yp)
        recv(f"OM{i - 1}", i, 1, H, H)
        send(f"OM{i}", i, 1, H + Q if last else H, Q if last else H, ym)
        if i == 1:
            dx_terms(1)
            recv("ZA", 0, 1, 0, H)
            cross(0, 1)
            y_part(0, 1)
            y_part(-1, 0)
        elif i == 2:
            recv("ZP1", -1, 1, 0, H)
            recv("ZM1", 1, 1, 0, H)
            cross(-1, 1)
            cross(1, 1)
            y_part(1, 0)
            dx_terms(2)
            dx_terms(3)
        else:
            lax.fori_loop(0, SUB, dx_first, 0)
            recv("ZP2", -2, 1, 0, H)
            recv("ZM2", 2, 1, 0, H)
            cross(-2, 1)
            cross(2, 1)
            y_part(-1, 1)
            y_part(1, 1)

    recv("PA3", -4, 0, 0, H)
    send("ZP4", -4, 0, 0, H, zp)
    recv("MB3", -4, 0, H, H)
    cross(-4, 0)
    dx_terms(4)
    recv("ZP3", -3, 1, 0, H)
    recv("ZM3", 3, 1, 0, H)
    cross(-3, 1)
    cross(3, 1)
    recv("OP3", -4, 1, H, Q)
    recv("OM3", -4, 1, H + Q, Q)
    dx_terms(5)
    other = lax.rem(c + 1, 2) * TOK
    part = ctall.at[pl.ds(other, TOK)]
    remote(part, part, cs.at[16], cr.at[16], core).wait_recv()
    for j in range(2):
        ctt[j] = ctall[:, j * BLK : (j + 1) * BLK].astype(F32).T.astype(BF16)
    y_part(-2, 0)
    recv("ZP4", -4, 1, 0, H)
    cross(-4, 1)
    dx_round(1)
    y_part(2, 0)

    for k, (dy, dzl) in enumerate(crossed):
        part = xpart(dy, dzl, 0, TOK, other)
        remote(part, part, cs.at[k], cr.at[k], core).wait_recv()
    from_gather = len(sent)

    def dw_term(tx, tzh, way):
        s = c * 32 + tx * 8 + tzh * 2 + way
        slot = table_ref[128 + s]
        return jnp.dot(ctt[slot & 1], xall[lax.shift_right_logical(slot, 5)], preferred_element_type=F32)

    def part_off(j):
        return lax.rem(2 + 3 * j - lax.div(j * (j - 1), 2), NZH)

    def dw_copy(o, j):
        return remote(wsb.at[o, j], wrb.at[o, j], ws.at[o, j], wr.at[o, j], xs_to[o])

    def dw_send(j, carry):
        tzh = lax.rem(zh + part_off(j), NZH)
        for o in (1, 0, 2):
            for i in range(2):
                encode(wsb.at[o, j, i], dw_term(lax.rem(x + o + 1, NX), tzh, i))
            dw_copy(o, j).start()
        return carry

    def wz_copy(j):
        return remote(zsb.at[j], zrb.at[j], wzs.at[j], wzr.at[j], zhs[(2, 1, 3)[j]])

    def dw_sum(j):
        tzh = lax.rem(zh + (2, 1, 3, 0)[j], NZH)
        for o in range(3):
            part = wrb.at[o, j]
            remote(part, part, ws.at[o, j], wr.at[o, j], core).wait_recv()
        for i in range(2):
            total = dw_term(x, tzh, i)
            for o in range(3):
                total = total + decode(wrb.at[o, j, i])
            if j < 3:
                encode(zsb.at[j, i], total)
            else:
                wf[i] = total
        if j < 3:
            wz_copy(j).start()

    lax.fori_loop(0, 4, dw_send, 0)
    dx_round(2)
    y_part(-3, 0)
    dw_sum(0)
    dx_round(3)
    dw_sum(1)
    dx_terms(6)
    dw_sum(2)
    dx_round(4)
    dw_sum(3)
    dx_terms(7)
    y_part(-4, 0)
    y_part(3, 0)
    dx_round(5)

    mine = c * 32 + x * 8 + zh * 2
    for j in (1, 2, 0):
        part = zrb.at[j]
        remote(part, part, wzs.at[j], wzr.at[j], core).wait_recv()
    for i in range(2):
        total = wf[i]
        for j in range(3):
            total = total + decode(zrb.at[j, i])
        total = jnp.where(mine + i < table_ref[192], total.T, jnp.zeros((BLK, BLK), F32))
        bgv[mine + i] = total.astype(BF16)

    def slots(dx, dzh, n=2, half=c):
        return bgv.at[pl.ds(half * 32 + lax.rem(x + dx + NX, NX) * 8 + lax.rem(zh + dzh + NZH, NZH) * 2, n)]

    def put(part, ss, rs, dev):
        copy = remote(part, part, ss, rs, dev)
        copy.start()
        sent.append(copy)

    def over(m, k):
        put(slots((0, -1, 1, 2)[m], -k), gcs.at[m, k], gcr.at[m, k], core)

    def gx_send(k):
        for way in (0, 1):
            put(slots(0, -k), gxs.at[way, k], gxr.at[way, k], xp if way == 0 else xm)

    def gx_pass(k):
        for way, dx in ((0, -1), (1, 1)):
            part = slots(dx, -k)
            remote(part, part, gxs.at[way, k], gxr.at[way, k], core).wait_recv()
            if (k in (0, 1)) == (way == 0):
                put(part, gfs.at[k], gfr.at[k], xp if way == 0 else xm)
            over(1 + way, k)

    def gf_take(k):
        part = slots(2, -k)
        remote(part, part, gfs.at[k], gfr.at[k], core).wait_recv()
        over(3, k)

    def write(half, m):
        part = pl.ds(half * 32 + lax.rem(x + (0, -1, 1, 2)[m] + NX, NX) * 8, 8)
        return pltpu.make_async_copy(bgv.at[part], bg_ref.at[part], os.at[(0 if half is c else 4) + m])

    for k in (2, 1, 3):
        put(slots(0, 0), gzs.at[k], gzr.at[k], zhs[k])
    gx_send(0)
    over(0, 0)
    for copy in sent[:from_gather]:
        copy.wait_send()
    dx_round(6)
    for k in (1, 3, 2):
        part = slots(0, -k)
        remote(part, part, gzs.at[k], gzr.at[k], core).wait_recv()
        gx_send(k)
        over(0, k)
        if k == 1:
            gx_pass(0)
    write(c, 0).start()

    def z_copy(j):
        return remote(dxb.at[1 - zl, 0, j], dxz.at[j], dzs.at[j], dzr.at[j], zp)

    for way in (0, 1):
        for j in range(SUB):
            dx_copy(way, 0, j).wait_send()
    for j in range(SUB):
        for way in (0, 1):
            dxf[way, j] = dx_part(way, 7, j)
        encode(dxb.at[1 - zl, 0, j], dxf[1 - zl, j])
        z_copy(j).start()
    gx_pass(1)
    gx_pass(3)
    y_part(-2, 1)
    y_part(2, 1)
    gx_pass(2)
    write(c, 1).start()
    write(c, 2).start()
    y_part(-3, 1)
    y_part(3, 1)
    y_part(-4, 1)
    youtv[...] = yacc[...].astype(BF16)
    ywrite = pltpu.make_async_copy(youtv, y_ref, os.at[8])
    ywrite.start()
    for j in range(SUB):
        part = dxz.at[j]
        remote(part, part, dzs.at[j], dzr.at[j], core).wait_recv()
        dxv[:, j * BLK : (j + 1) * BLK] = (dxf[zl, j] + decode(part)).astype(BF16)
    dxwrite = pltpu.make_async_copy(dxv, dx_ref, os.at[9])
    dxwrite.start()
    for k in (0, 1, 3, 2):
        gf_take(k)
    write(c, 3).start()
    for m in range(4):
        for k in range(4):
            part = slots((0, -1, 1, 2)[m], -k, 2, 1 - c)
            remote(part, part, gcs.at[m, k], gcr.at[m, k], core).wait_recv()
        write(1 - c, m).start()

    for copy in sent[from_gather:]:
        copy.wait_send()
    for j in range(SUB):
        z_copy(j).wait_send()
    for j in range(3):
        wz_copy(j).wait_send()

    for way in (0, 1):

        def left(n, carry, way=way):
            dx_copy(way, lax.div(n, SUB), lax.rem(n, SUB)).wait_send()
            return carry

        lax.fori_loop(SUB, 7 * SUB, left, 0)
    for o in range(3):

        def gone(j, carry, o=o):
            dw_copy(o, j).wait_send()
            return carry

        lax.fori_loop(0, 4, gone, 0)
    for m in range(4):
        write(c, m).wait()
        write(1 - c, m).wait()
    ywrite.wait()
    dxwrite.wait()


def per_device(tokens, cotangent, blocks, slot_block, shard_count):
    cell = slot_block // 32 * 2 + slot_block % 2
    place = jnp.arange(64, dtype=jnp.int32)
    here = (cell[:, None] == jnp.arange(128, dtype=jnp.int32)[None, :]) & (place < shard_count[0])[:, None]
    cell_slot = jnp.max(jnp.where(here, place[:, None], -1), axis=0)
    table = jnp.concatenate([cell_slot, slot_block, shard_count])
    smem, hbm = pl.BlockSpec(memory_space=pltpu.SMEM), pl.BlockSpec(memory_space=pltpu.HBM)
    dma = pltpu.SemaphoreType.DMA
    return pl.pallas_call(
        kernel,
        out_shape=(
            jax.ShapeDtypeStruct((TOK, CF), BF16),
            jax.ShapeDtypeStruct((TOK, XF), BF16),
            jax.ShapeDtypeStruct((64, BLK, BLK), BF16),
        ),
        in_specs=[smem] + [hbm] * 3,
        out_specs=(hbm,) * 3,
        scratch_shapes=[
            pltpu.VMEM((64, 2 * TOK, BLK), BF16),
            pltpu.VMEM((2 * TOK, CF), BF16),
            pltpu.VMEM((2, BLK, 2 * TOK), BF16),
            pltpu.VMEM((64, BLK, BLK), BF16),
            pltpu.VMEM((64 * BLK, CF), BF16),
            pltpu.VMEM((TOK, CF), F32),
            pltpu.VMEM((2, 8, SUB, BLK, BLK), F32),
            pltpu.VMEM((2, 8, SUB, CODE, BLK), jnp.int32),
            pltpu.VMEM((2, SUB, BLK, BLK), F32),
            pltpu.VMEM((SUB, CODE, BLK), jnp.int32),
            pltpu.VMEM((3, 4, 2, CODE, BLK), jnp.int32),
            pltpu.VMEM((3, 4, 2, CODE, BLK), jnp.int32),
            pltpu.VMEM((2, BLK, BLK), F32),
            pltpu.VMEM((3, 2, CODE, BLK), jnp.int32),
            pltpu.VMEM((3, 2, CODE, BLK), jnp.int32),
            pltpu.VMEM((64, BLK, BLK), BF16),
            pltpu.VMEM((TOK, CF), BF16),
            pltpu.VMEM((TOK, XF), BF16),
            dma((6,)), dma((40,)), dma((40,)), dma((17,)), dma((17,)),
            dma((2, 8, SUB)), dma((2, 8, SUB)), dma((SUB,)), dma((SUB,)),
            dma((3, 4)), dma((3, 4)), dma((3,)), dma((3,)),
            dma((4,)), dma((4,)), dma((2, 4)), dma((2, 4)), dma((4,)), dma((4,)), dma((4, 4)), dma((4, 4)), dma((10,)),
        ],
        compiler_params=pltpu.CompilerParams(
            collective_id=0, has_side_effects=True, vmem_limit_bytes=50 << 20
        ),
    )(table, tokens, cotangent, blocks)


def solution(mesh):
    return jax.shard_map(
        per_device,
        mesh=mesh,
        in_specs=(P("dp", "fsdp"), P("dp", "fsdp"), P("fsdp", None, None), P("fsdp"), P("fsdp")),
        out_specs=(P("dp", "fsdp"), P("dp", "fsdp"), P("fsdp", None, None)),
        check_vma=False,
    )
```

```python
import functools

import jax
import jax.numpy as jnp
from jax import lax
from jax.experimental import pallas as pl
from jax.experimental.pallas import tpu as pltpu
from jax.sharding import PartitionSpec as P

BLK = 128
NY, NZL, NX, NZH = 8, 2, 4, 4
TOK = 128
XF = 512
CF = 256
SUB = 4
MESH = pl.DeviceIdType.MESH
F32, BF16 = jnp.float32, jnp.bfloat16


CODE = 72
STEPS = 32760.0


def encode(ref, value):
    tiles = value.reshape(16, 8, BLK)
    top = jnp.max(jnp.abs(tiles), axis=0)
    power = jnp.ceil(jnp.log2(jnp.maximum(top, 1e-33)) * 8.0)
    code = jnp.round(tiles * (jnp.exp2(power * -0.125) * STEPS)[None]).astype(jnp.int32)
    pairs = lax.shift_left(code[:8], jnp.full((8, 8, BLK), 16, jnp.int32)) | (code[8:] & 0xFFFF)
    ref[0:64, :] = pairs.reshape(64, BLK)
    ref[64:CODE, :] = power.astype(jnp.int32)


def decode(ref):
    pairs = ref[0:64, :].reshape(8, 8, BLK)
    scale = jnp.exp2(ref[64:CODE, :].astype(F32) * 0.125) * (1.0 / STEPS)
    by = jnp.full((8, 8, BLK), 16, jnp.int32)
    high = lax.shift_right_arithmetic(pairs, by)
    low = lax.shift_right_arithmetic(lax.shift_left(pairs, by), by)
    tiles = jnp.concatenate([high, low], axis=0).astype(F32) * scale[None]
    return tiles.reshape(BLK, BLK)


def kernel(
    table_ref, tok_hbm, ct_hbm, blk_hbm,
    y_ref, dx_ref, bg_ref,
    xall, ctall, ctt, blk_ref, wd, yacc, dxt, dxb, dxf, dxz, wsb, wrb, wf, zsb, zrb,
    ls, xs, xr, cs, cr, dxs, dxr, dzs, dzr, ws, wr, wzs, wzr, gzs, gzr, gxs, gxr, gfs, gfr, gcs, gcr,
):
    d, f = lax.axis_index("dp"), lax.axis_index("fsdp")
    zh, x, c = lax.div(d, 8), lax.rem(lax.div(d, 2), 4), lax.rem(d, 2)
    y, zl = lax.div(f, 2), lax.rem(f, 2)

    def at(dzh=0, dx=0, dc=0, dy=0, dzl=0):
        nzh, nx = lax.rem(zh + dzh + NZH, NZH), lax.rem(x + dx + NX, NX)
        nc, ny, nzl = lax.rem(c + dc, 2), lax.rem(y + dy + NY, NY), lax.rem(zl + dzl, 2)
        return ((nzh * 4 + nx) * 2 + nc, ny * 2 + nzl)

    yp, ym, zp, xp, xm = at(dy=1), at(dy=-1), at(dzl=1), at(dx=1), at(dx=-1)
    core = at(dc=1)
    zhs = [None, at(dzh=1), at(dzh=2), at(dzh=3)]
    xs_to = [xp, at(dx=2), xm]
    base = c * TOK

    barrier = pltpu.get_barrier_semaphore()
    for peer in (yp, ym, zp, *xs_to, core, *zhs[1:]):
        pl.semaphore_signal(barrier, inc=1, device_id=peer, device_id_type=MESH)

    loads = [
        pltpu.make_async_copy(tok_hbm.at[:, pl.ds(b * BLK, BLK)], xall.at[4 * f + b, pl.ds(base, TOK)], ls.at[b])
        for b in range(4)
    ]
    loads.append(pltpu.make_async_copy(ct_hbm, ctall.at[pl.ds(base, TOK)], ls.at[4]))
    loads.append(pltpu.make_async_copy(blk_hbm, blk_ref, ls.at[5]))
    for load in loads:
        load.start()

    def remote(src, dst, ss, rs, dev):
        return pltpu.make_async_remote_copy(
            src_ref=src, dst_ref=dst, send_sem=ss, recv_sem=rs, device_id=dev, device_id_type=MESH
        )

    names = {}
    sent = []

    def src_f(dy, dzl):
        return lax.rem(y + dy + NY, NY) * 2 + lax.rem(zl + dzl, 2)

    def xpart(dy, dzl, r0, n, start=base):
        return xall.at[pl.ds(4 * src_f(dy, dzl), 4), pl.ds(start + r0, n), :]

    def send(name, dy, dzl, r0, n, dev):
        k = names.setdefault(name, len(names))
        part = xpart(dy, dzl, r0, n)
        copy = remote(part, part, xs.at[k], xr.at[k], dev)
        copy.start()
        sent.append(copy)

    def recv(name, dy, dzl, r0, n):
        k = names[name]
        part = xpart(dy, dzl, r0, n)
        remote(part, part, xs.at[k], xr.at[k], core).wait_recv()

    crossed = []

    def cross(dy, dzl):
        k = len(crossed)
        part = xpart(dy, dzl, 0, TOK)
        copy = remote(part, part, cs.at[k], cr.at[k], core)
        copy.start()
        sent.append(copy)
        crossed.append((dy, dzl))

    H = TOK // 2
    Q = TOK // 4
    for load in loads[:5]:
        load.wait()
    pl.semaphore_wait(barrier, 10)
    send("Z0", 0, 0, H, H, zp)
    send("PA0", 0, 0, 0, H, yp)
    send("MA0", 0, 0, 0, H, ym)
    send("PB0", 0, 0, H, H, yp)
    send("MB0", 0, 0, H, H, ym)
    send("ZA", 0, 0, 0, H, zp)
    ctpart = ctall.at[pl.ds(base, TOK)]
    ctcopy = remote(ctpart, ctpart, cs.at[16], cr.at[16], core)
    ctcopy.start()
    sent.append(ctcopy)
    cross(0, 0)
    loads[5].wait()

    def build(r, carry):
        for j in range(2):
            m = table_ref[2 * r + j]
            b = blk_ref[jnp.maximum(m, 0)]
            b = jnp.where(m >= 0, b, jnp.zeros_like(b))
            wd[pl.ds(pl.multiple_of(r * BLK, BLK), BLK), j * BLK : (j + 1) * BLK] = b
        return carry

    def dx_target(way, s):
        return lax.rem(y - 1 - s + 2 * NY, NY) if way == 0 else lax.rem(y + 1 + s, NY)

    def dx_terms(s):
        for way in (0, 1):
            rows = pl.multiple_of(dx_target(way, s) * (2 * XF) + way * XF, XF)
            terms = lax.dot_general(
                ctall[pl.ds(base, TOK), :], wd[pl.ds(rows, XF), :], (((1,), (1,)), ((), ())), preferred_element_type=F32
            )
            for j in range(SUB):
                dxt[way, s, j] = terms[:, j * BLK : (j + 1) * BLK]

    def dx_copy(way, s, j):
        return remote(
            dxb.at[way, s, j], dxb.at[way, s + 1, j], dxs.at[way, s, j], dxr.at[way, s + 1, j],
            yp if way == 0 else ym,
        )

    def dx_part(way, s, j):
        part = dxb.at[way, s, j]
        remote(part, part, dxs.at[way, 0, j], dxr.at[way, s, j], core).wait_recv()
        return dxt[way, s, j] + decode(part)

    def dx_first(j, carry):
        for way in (0, 1):
            encode(dxb.at[way, 0, j], dxt[way, 0, j])
            dx_copy(way, 0, j).start()
        return carry

    def dx_round(s):
        def step(j, carry):
            for way in (0, 1):
                encode(dxb.at[way, s, j], dx_part(way, s, j))
                dx_copy(way, s, j).start()
            return carry

        lax.fori_loop(0, SUB, step, 0)

    def y_part(dy, dzl, first=False):
        k = src_f(dy, dzl)
        xb = jnp.concatenate([xall[4 * k + b, pl.ds(base, TOK), :] for b in range(4)], axis=1)
        rows = pl.ds(pl.multiple_of(k * XF, XF), XF)
        term = jnp.dot(xb, wd[rows, :], preferred_element_type=F32)
        yacc[...] = term if first else yacc[...] + term

    lax.fori_loop(0, 64, build, 0)
    y_part(0, 0, True)
    recv("Z0", 0, 1, H, H)
    send("OP0", 0, 1, H, H, yp)
    send("OM0", 0, 1, H, H, ym)
    dx_terms(0)
    for i in (1, 2, 3):
        last = i == 3
        recv(f"PA{i - 1}", -i, 0, 0, H)
        send(f"PA{i}", -i, 0, 0, H, yp)
        send(f"ZP{i}", -i, 0, 0, H, zp)
        recv(f"MA{i - 1}", i, 0, 0, H)
        if not last:
            send(f"MA{i}", i, 0, 0, H, ym)
        send(f"ZM{i}", i, 0, 0, H, zp)
        recv(f"PB{i - 1}", -i, 0, H, H)
        if not last:
            send(f"PB{i}", -i, 0, H, H, yp)
        recv(f"MB{i - 1}", i, 0, H, H)
        send(f"MB{i}", i, 0, H, H, ym)
        cross(-i, 0)
        cross(i, 0)
        recv(f"OP{i - 1}", -i, 1, H, H)
        send(f"OP{i}", -i, 1, H, Q if last else H, yp)
        recv(f"OM{i - 1}", i, 1, H, H)
        send(f"OM{i}", i, 1, H + Q if last else H, Q if last else H, ym)
        if i == 1:
            dx_terms(1)
            recv("ZA", 0, 1, 0, H)
            cross(0, 1)
            y_part(0, 1)
            y_part(-1, 0)
        elif i == 2:
            recv("ZP1", -1, 1, 0, H)
            recv("ZM1", 1, 1, 0, H)
            cross(-1, 1)
            cross(1, 1)
            y_part(1, 0)
            dx_terms(2)
            dx_terms(3)
        else:
            lax.fori_loop(0, SUB, dx_first, 0)
            recv("ZP2", -2, 1, 0, H)
            recv("ZM2", 2, 1, 0, H)
            cross(-2, 1)
            cross(2, 1)
            y_part(-1, 1)
            y_part(1, 1)

    recv("PA3", -4, 0, 0, H)
    send("ZP4", -4, 0, 0, H, zp)
    recv("MB3", -4, 0, H, H)
    cross(-4, 0)
    dx_terms(4)
    recv("ZP3", -3, 1, 0, H)
    recv("ZM3", 3, 1, 0, H)
    cross(-3, 1)
    cross(3, 1)
    recv("OP3", -4, 1, H, Q)
    recv("OM3", -4, 1, H + Q, Q)
    dx_terms(5)
    other = lax.rem(c + 1, 2) * TOK
    part = ctall.at[pl.ds(other, TOK)]
    remote(part, part, cs.at[16], cr.at[16], core).wait_recv()
    for j in range(2):
        ctt[j] = ctall[:, j * BLK : (j + 1) * BLK].astype(F32).T.astype(BF16)
    y_part(-2, 0)
    recv("ZP4", -4, 1, 0, H)
    cross(-4, 1)
    dx_round(1)
    y_part(2, 0)

    for k, (dy, dzl) in enumerate(crossed):
        part = xpart(dy, dzl, 0, TOK, other)
        remote(part, part, cs.at[k], cr.at[k], core).wait_recv()
    from_gather = len(sent)

    def dw_term(tx, tzh, way):
        s = c * 32 + tx * 8 + tzh * 2 + way
        slot = table_ref[128 + s]
        return jnp.dot(ctt[slot & 1], xall[lax.shift_right_logical(slot, 5)], preferred_element_type=F32)

    def part_off(j):
        return lax.rem(2 + 3 * j - lax.div(j * (j - 1), 2), NZH)

    def dw_copy(o, j):
        return remote(wsb.at[o, j], wrb.at[o, j], ws.at[o, j], wr.at[o, j], xs_to[o])

    def dw_send(j, carry):
        tzh = lax.rem(zh + part_off(j), NZH)
        for o in (1, 0, 2):
            for i in range(2):
                encode(wsb.at[o, j, i], dw_term(lax.rem(x + o + 1, NX), tzh, i))
            dw_copy(o, j).start()
        return carry

    def wz_copy(j):
        return remote(zsb.at[j], zrb.at[j], wzs.at[j], wzr.at[j], zhs[(2, 1, 3)[j]])

    def dw_sum(j):
        tzh = lax.rem(zh + (2, 1, 3, 0)[j], NZH)
        for o in range(3):
            part = wrb.at[o, j]
            remote(part, part, ws.at[o, j], wr.at[o, j], core).wait_recv()
        for i in range(2):
            total = dw_term(x, tzh, i)
            for o in range(3):
                total = total + decode(wrb.at[o, j, i])
            if j < 3:
                encode(zsb.at[j, i], total)
            else:
                wf[i] = total
        if j < 3:
            wz_copy(j).start()

    lax.fori_loop(0, 4, dw_send, 0)
    dx_round(2)
    y_part(-3, 0)
    dw_sum(0)
    dx_round(3)
    dw_sum(1)
    dx_terms(6)
    dw_sum(2)
    dx_round(4)
    dw_sum(3)
    dx_terms(7)
    y_part(-4, 0)
    y_part(3, 0)
    dx_round(5)

    mine = c * 32 + x * 8 + zh * 2
    for j in (1, 2, 0):
        part = zrb.at[j]
        remote(part, part, wzs.at[j], wzr.at[j], core).wait_recv()
    for i in range(2):
        total = wf[i]
        for j in range(3):
            total = total + decode(zrb.at[j, i])
        total = jnp.where(mine + i < table_ref[192], total.T, jnp.zeros((BLK, BLK), F32))
        bg_ref[mine + i] = total.astype(BF16)

    def slots(dx, dzh, n=2, half=c):
        return bg_ref.at[pl.ds(half * 32 + lax.rem(x + dx + NX, NX) * 8 + lax.rem(zh + dzh + NZH, NZH) * 2, n)]

    def put(part, ss, rs, dev):
        copy = remote(part, part, ss, rs, dev)
        copy.start()
        sent.append(copy)

    def over(m, k):
        put(slots((0, -1, 1, 2)[m], -k), gcs.at[m, k], gcr.at[m, k], core)

    def gx_send(k):
        for way in (0, 1):
            put(slots(0, -k), gxs.at[way, k], gxr.at[way, k], xp if way == 0 else xm)

    def gx_pass(k):
        for way, dx in ((0, -1), (1, 1)):
            part = slots(dx, -k)
            remote(part, part, gxs.at[way, k], gxr.at[way, k], core).wait_recv()
            if (k in (0, 1)) == (way == 0):
                put(part, gfs.at[k], gfr.at[k], xp if way == 0 else xm)
            over(1 + way, k)

    def gf_take(k):
        part = slots(2, -k)
        remote(part, part, gfs.at[k], gfr.at[k], core).wait_recv()
        over(3, k)

    for k in (2, 1, 3):
        put(slots(0, 0), gzs.at[k], gzr.at[k], zhs[k])
    gx_send(0)
    over(0, 0)
    for copy in sent[:from_gather]:
        copy.wait_send()
    dx_round(6)
    for k in (1, 3, 2):
        part = slots(0, -k)
        remote(part, part, gzs.at[k], gzr.at[k], core).wait_recv()
        gx_send(k)
        over(0, k)
        if k == 1:
            gx_pass(0)

    def z_copy(j):
        return remote(dxb.at[1 - zl, 0, j], dxz.at[j], dzs.at[j], dzr.at[j], zp)

    for way in (0, 1):
        for j in range(SUB):
            dx_copy(way, 0, j).wait_send()
    for j in range(SUB):
        for way in (0, 1):
            dxf[way, j] = dx_part(way, 7, j)
        encode(dxb.at[1 - zl, 0, j], dxf[1 - zl, j])
        z_copy(j).start()
    gx_pass(1)
    gx_pass(3)
    y_part(-2, 1)
    y_part(2, 1)
    gx_pass(2)
    y_part(-3, 1)
    y_part(3, 1)
    y_part(-4, 1)
    y_ref[...] = yacc[...].astype(BF16)
    for j in range(SUB):
        part = dxz.at[j]
        remote(part, part, dzs.at[j], dzr.at[j], core).wait_recv()
        dx_ref[:, j * BLK : (j + 1) * BLK] = (dxf[zl, j] + decode(part)).astype(BF16)
    for j in range(3):
        wz_copy(j).wait_send()

    for way in (0, 1):

        def left(n, carry, way=way):
            dx_copy(way, lax.div(n, SUB), lax.rem(n, SUB)).wait_send()
            return carry

        lax.fori_loop(SUB, 7 * SUB, left, 0)
    for o in range(3):

        def gone(j, carry, o=o):
            dw_copy(o, j).wait_send()
            return carry

        lax.fori_loop(0, 4, gone, 0)

    for k in (0, 1, 3, 2):
        gf_take(k)
    for m in range(4):
        for k in range(4):
            part = slots((0, -1, 1, 2)[m], -k, 2, 1 - c)
            remote(part, part, gcs.at[m, k], gcr.at[m, k], core).wait_recv()

    for copy in sent[from_gather:]:
        copy.wait_send()
    for j in range(SUB):
        z_copy(j).wait_send()


def per_device(tokens, cotangent, blocks, slot_block, shard_count):
    n = jnp.arange(193, dtype=jnp.int32)[:, None]
    place = jnp.arange(64, dtype=jnp.int32)[None, :]
    block = n // 2 * 32 + lax.axis_index("fsdp") * 2 + n % 2
    held = (slot_block[None, :] == block) & (place < shard_count[0])
    entry = jnp.where(n < 128, jnp.where(held, place, -1), jnp.where(place == n - 128, slot_block[None, :], -1))
    table = jnp.max(jnp.where(n < 192, entry, shard_count[0]), axis=1)
    smem, vmem, hbm = (pl.BlockSpec(memory_space=m) for m in (pltpu.SMEM, pltpu.VMEM, pltpu.HBM))
    dma = pltpu.SemaphoreType.DMA
    return pl.pallas_call(
        kernel,
        out_shape=(
            jax.ShapeDtypeStruct((TOK, CF), BF16),
            jax.ShapeDtypeStruct((TOK, XF), BF16),
            jax.ShapeDtypeStruct((64, BLK, BLK), BF16),
        ),
        in_specs=[smem] + [hbm] * 3,
        out_specs=(vmem,) * 3,
        scratch_shapes=[
            pltpu.VMEM((64, 2 * TOK, BLK), BF16),
            pltpu.VMEM((2 * TOK, CF), BF16),
            pltpu.VMEM((2, BLK, 2 * TOK), BF16),
            pltpu.VMEM((64, BLK, BLK), BF16),
            pltpu.VMEM((64 * BLK, CF), BF16),
            pltpu.VMEM((TOK, CF), F32),
            pltpu.VMEM((2, 8, SUB, BLK, BLK), F32),
            pltpu.VMEM((2, 8, SUB, CODE, BLK), jnp.int32),
            pltpu.VMEM((2, SUB, BLK, BLK), F32),
            pltpu.VMEM((SUB, CODE, BLK), jnp.int32),
            pltpu.VMEM((3, 4, 2, CODE, BLK), jnp.int32),
            pltpu.VMEM((3, 4, 2, CODE, BLK), jnp.int32),
            pltpu.VMEM((2, BLK, BLK), F32),
            pltpu.VMEM((3, 2, CODE, BLK), jnp.int32),
            pltpu.VMEM((3, 2, CODE, BLK), jnp.int32),
            dma((6,)), dma((40,)), dma((40,)), dma((17,)), dma((17,)),
            dma((2, 8, SUB)), dma((2, 8, SUB)), dma((SUB,)), dma((SUB,)),
            dma((3, 4)), dma((3, 4)), dma((3,)), dma((3,)),
            dma((4,)), dma((4,)), dma((2, 4)), dma((2, 4)), dma((4,)), dma((4,)), dma((4, 4)), dma((4, 4)),
        ],
        compiler_params=pltpu.CompilerParams(
            collective_id=0, has_side_effects=True, vmem_limit_bytes=50 << 20
        ),
    )(table, tokens, cotangent, blocks)


def solution(mesh):
    return jax.shard_map(
        per_device,
        mesh=mesh,
        in_specs=(P("dp", "fsdp"), P("dp", "fsdp"), P("fsdp", None, None), P("fsdp"), P("fsdp")),
        out_specs=(P("dp", "fsdp"), P("dp", "fsdp"), P("fsdp", None, None)),
        check_vma=False,
    )
```

```python
import functools

import jax
import jax.numpy as jnp
from jax import lax
from jax.experimental import pallas as pl
from jax.experimental.pallas import tpu as pltpu
from jax.sharding import PartitionSpec as P

BLK = 128
NY, NZL, NX, NZH = 8, 2, 4, 4
TOK = 128
XF = 512
CF = 256
SUB = 4
MESH = pl.DeviceIdType.MESH
F32, BF16 = jnp.float32, jnp.bfloat16


CODE = 72
STEPS = 32760.0


def encode(ref, value):
    tiles = value.reshape(16, 8, BLK)
    top = jnp.max(jnp.abs(tiles), axis=0)
    power = jnp.ceil(jnp.log2(jnp.maximum(top, 1e-33)) * 8.0)
    code = jnp.round(tiles * (jnp.exp2(power * -0.125) * STEPS)[None]).astype(jnp.int32)
    pairs = lax.shift_left(code[:8], jnp.full((8, 8, BLK), 16, jnp.int32)) | (code[8:] & 0xFFFF)
    ref[0:64, :] = pairs.reshape(64, BLK)
    ref[64:CODE, :] = power.astype(jnp.int32)


def decode(ref):
    pairs = ref[0:64, :].reshape(8, 8, BLK)
    scale = jnp.exp2(ref[64:CODE, :].astype(F32) * 0.125) * (1.0 / STEPS)
    by = jnp.full((8, 8, BLK), 16, jnp.int32)
    high = lax.shift_right_arithmetic(pairs, by)
    low = lax.shift_right_arithmetic(lax.shift_left(pairs, by), by)
    tiles = jnp.concatenate([high, low], axis=0).astype(F32) * scale[None]
    return tiles.reshape(BLK, BLK)


def kernel(
    table_ref, tok_hbm, ct_hbm, blk_hbm,
    y_ref, dx_ref, bg_ref,
    xall, ctall, ctt, blk_ref, wd, yacc, dxt, dxb, dxf, dxz, wsb, wrb, wf, zsb, zrb,
    ls, xs, xr, cs, cr, dxs, dxr, dzs, dzr, ws, wr, wzs, wzr, gzs, gzr, gxs, gxr, gfs, gfr, gcs, gcr,
):
    d, f = lax.axis_index("dp"), lax.axis_index("fsdp")
    zh, x, c = lax.div(d, 8), lax.rem(lax.div(d, 2), 4), lax.rem(d, 2)
    y, zl = lax.div(f, 2), lax.rem(f, 2)

    def at(dzh=0, dx=0, dc=0, dy=0, dzl=0):
        nzh, nx = lax.rem(zh + dzh + NZH, NZH), lax.rem(x + dx + NX, NX)
        nc, ny, nzl = lax.rem(c + dc, 2), lax.rem(y + dy + NY, NY), lax.rem(zl + dzl, 2)
        return ((nzh * 4 + nx) * 2 + nc, ny * 2 + nzl)

    yp, ym, zp, xp, xm = at(dy=1), at(dy=-1), at(dzl=1), at(dx=1), at(dx=-1)
    core = at(dc=1)
    zhs = [None, at(dzh=1), at(dzh=2), at(dzh=3)]
    xs_to = [xp, at(dx=2), xm]
    base = c * TOK

    barrier = pltpu.get_barrier_semaphore()
    for peer in (yp, ym, zp, *xs_to, core, *zhs[1:]):
        pl.semaphore_signal(barrier, inc=1, device_id=peer, device_id_type=MESH)

    loads = [
        pltpu.make_async_copy(tok_hbm.at[:, pl.ds(b * BLK, BLK)], xall.at[4 * f + b, pl.ds(base, TOK)], ls.at[b])
        for b in range(4)
    ]
    loads.append(pltpu.make_async_copy(ct_hbm, ctall.at[pl.ds(base, TOK)], ls.at[4]))
    loads.append(pltpu.make_async_copy(blk_hbm, blk_ref, ls.at[5]))
    for load in loads:
        load.start()

    def remote(src, dst, ss, rs, dev):
        return pltpu.make_async_remote_copy(
            src_ref=src, dst_ref=dst, send_sem=ss, recv_sem=rs, device_id=dev, device_id_type=MESH
        )

    names = {}
    sent = []

    def src_f(dy, dzl):
        return lax.rem(y + dy + NY, NY) * 2 + lax.rem(zl + dzl, 2)

    def xpart(dy, dzl, r0, n, start=base):
        return xall.at[pl.ds(4 * src_f(dy, dzl), 4), pl.ds(start + r0, n), :]

    def send(name, dy, dzl, r0, n, dev):
        k = names.setdefault(name, len(names))
        part = xpart(dy, dzl, r0, n)
        copy = remote(part, part, xs.at[k], xr.at[k], dev)
        copy.start()
        sent.append(copy)

    def recv(name, dy, dzl, r0, n):
        k = names[name]
        part = xpart(dy, dzl, r0, n)
        remote(part, part, xs.at[k], xr.at[k], core).wait_recv()

    crossed = []

    def cross(dy, dzl):
        k = len(crossed)
        part = xpart(dy, dzl, 0, TOK)
        copy = remote(part, part, cs.at[k], cr.at[k], core)
        copy.start()
        sent.append(copy)
        crossed.append((dy, dzl))

    H = TOK // 2
    Q = TOK // 4
    for load in loads[:5]:
        load.wait()
    pl.semaphore_wait(barrier, 10)
    send("Z0", 0, 0, H, H, zp)
    send("PA0", 0, 0, 0, H, yp)
    send("MA0", 0, 0, 0, H, ym)
    send("PB0", 0, 0, H, H, yp)
    send("MB0", 0, 0, H, H, ym)
    send("ZA", 0, 0, 0, H, zp)
    ctpart = ctall.at[pl.ds(base, TOK)]
    ctcopy = remote(ctpart, ctpart, cs.at[16], cr.at[16], core)
    ctcopy.start()
    sent.append(ctcopy)
    cross(0, 0)
    loads[5].wait()

    def build(r, carry):
        for j in range(2):
            m = table_ref[2 * r + j]
            b = blk_ref[jnp.maximum(m, 0)]
            b = jnp.where(m >= 0, b, jnp.zeros_like(b))
            wd[pl.ds(pl.multiple_of(r * BLK, BLK), BLK), j * BLK : (j + 1) * BLK] = b
        return carry

    def dx_target(way, s):
        return lax.rem(y - 1 - s + 2 * NY, NY) if way == 0 else lax.rem(y + 1 + s, NY)

    def dx_terms(s):
        for way in (0, 1):
            rows = pl.multiple_of(dx_target(way, s) * (2 * XF) + way * XF, XF)
            terms = lax.dot_general(
                ctall[pl.ds(base, TOK), :], wd[pl.ds(rows, XF), :], (((1,), (1,)), ((), ())), preferred_element_type=F32
            )
            for j in range(SUB):
                dxt[way, s, j] = terms[:, j * BLK : (j + 1) * BLK]

    def dx_copy(way, s, j):
        return remote(
            dxb.at[way, s, j], dxb.at[way, s + 1, j], dxs.at[way, s, j], dxr.at[way, s + 1, j],
            yp if way == 0 else ym,
        )

    def dx_part(way, s, j):
        part = dxb.at[way, s, j]
        remote(part, part, dxs.at[way, 0, j], dxr.at[way, s, j], core).wait_recv()
        return dxt[way, s, j] + decode(part)

    def dx_first(j, carry):
        for way in (0, 1):
            encode(dxb.at[way, 0, j], dxt[way, 0, j])
            dx_copy(way, 0, j).start()
        return carry

    def dx_round(s):
        def step(j, carry):
            for way in (0, 1):
                encode(dxb.at[way, s, j], dx_part(way, s, j))
                dx_copy(way, s, j).start()
            return carry

        lax.fori_loop(0, SUB, step, 0)

    def y_part(dy, dzl, first=False):
        k = src_f(dy, dzl)
        xb = jnp.concatenate([xall[4 * k + b, pl.ds(base, TOK), :] for b in range(4)], axis=1)
        rows = pl.ds(pl.multiple_of(k * XF, XF), XF)
        term = jnp.dot(xb, wd[rows, :], preferred_element_type=F32)
        yacc[...] = term if first else yacc[...] + term

    lax.fori_loop(0, 64, build, 0)
    y_part(0, 0, True)
    recv("Z0", 0, 1, H, H)
    send("OP0", 0, 1, H, H, yp)
    send("OM0", 0, 1, H, H, ym)
    dx_terms(0)
    for i in (1, 2, 3):
        last = i == 3
        recv(f"PA{i - 1}", -i, 0, 0, H)
        send(f"PA{i}", -i, 0, 0, H, yp)
        send(f"ZP{i}", -i, 0, 0, H, zp)
        recv(f"MA{i - 1}", i, 0, 0, H)
        if not last:
            send(f"MA{i}", i, 0, 0, H, ym)
        send(f"ZM{i}", i, 0, 0, H, zp)
        recv(f"PB{i - 1}", -i, 0, H, H)
        if not last:
            send(f"PB{i}", -i, 0, H, H, yp)
        recv(f"MB{i - 1}", i, 0, H, H)
        send(f"MB{i}", i, 0, H, H, ym)
        cross(-i, 0)
        cross(i, 0)
        recv(f"OP{i - 1}", -i, 1, H, H)
        send(f"OP{i}", -i, 1, H, Q if last else H, yp)
        recv(f"OM{i - 1}", i, 1, H, H)
        send(f"OM{i}", i, 1, H + Q if last else H, Q if last else H, ym)
        if i == 1:
            dx_terms(1)
            recv("ZA", 0, 1, 0, H)
            cross(0, 1)
            y_part(0, 1)
            y_part(-1, 0)
        elif i == 2:
            recv("ZP1", -1, 1, 0, H)
            recv("ZM1", 1, 1, 0, H)
            cross(-1, 1)
            cross(1, 1)
            y_part(1, 0)
            dx_terms(2)
            dx_terms(3)
        else:
            lax.fori_loop(0, SUB, dx_first, 0)
            recv("ZP2", -2, 1, 0, H)
            recv("ZM2", 2, 1, 0, H)
            cross(-2, 1)
            cross(2, 1)
            y_part(-1, 1)
            y_part(1, 1)

    recv("PA3", -4, 0, 0, H)
    send("ZP4", -4, 0, 0, H, zp)
    recv("MB3", -4, 0, H, H)
    cross(-4, 0)
    dx_terms(4)
    recv("ZP3", -3, 1, 0, H)
    recv("ZM3", 3, 1, 0, H)
    cross(-3, 1)
    cross(3, 1)
    recv("OP3", -4, 1, H, Q)
    recv("OM3", -4, 1, H + Q, Q)
    dx_terms(5)
    other = lax.rem(c + 1, 2) * TOK
    part = ctall.at[pl.ds(other, TOK)]
    remote(part, part, cs.at[16], cr.at[16], core).wait_recv()
    for j in range(2):
        ctt[j] = ctall[:, j * BLK : (j + 1) * BLK].astype(F32).T.astype(BF16)
    y_part(-2, 0)
    recv("ZP4", -4, 1, 0, H)
    cross(-4, 1)
    dx_round(1)
    y_part(2, 0)

    for k, (dy, dzl) in enumerate(crossed):
        part = xpart(dy, dzl, 0, TOK, other)
        remote(part, part, cs.at[k], cr.at[k], core).wait_recv()
    from_gather = len(sent)

    def dw_term(tx, tzh, way):
        s = c * 32 + tx * 8 + tzh * 2 + way
        slot = table_ref[128 + s]
        return jnp.dot(ctt[slot & 1], xall[lax.shift_right_logical(slot, 5)], preferred_element_type=F32)

    def part_off(j):
        return lax.rem(2 + 3 * j - lax.div(j * (j - 1), 2), NZH)

    def dw_copy(o, j):
        return remote(wsb.at[o, j], wrb.at[o, j], ws.at[o, j], wr.at[o, j], xs_to[o])

    def dw_send(j, carry):
        tzh = lax.rem(zh + part_off(j), NZH)
        for o in (1, 0, 2):
            for i in range(2):
                encode(wsb.at[o, j, i], dw_term(lax.rem(x + o + 1, NX), tzh, i))
            dw_copy(o, j).start()
        return carry

    def wz_copy(j):
        return remote(zsb.at[j], zrb.at[j], wzs.at[j], wzr.at[j], zhs[(2, 1, 3)[j]])

    def dw_sum(j):
        tzh = lax.rem(zh + (2, 1, 3, 0)[j], NZH)
        for o in range(3):
            part = wrb.at[o, j]
            remote(part, part, ws.at[o, j], wr.at[o, j], core).wait_recv()
        for i in range(2):
            total = dw_term(x, tzh, i)
            for o in range(3):
                total = total + decode(wrb.at[o, j, i])
            if j < 3:
                encode(zsb.at[j, i], total)
            else:
                wf[i] = total
        if j < 3:
            wz_copy(j).start()

    lax.fori_loop(0, 2, dw_send, 0)
    dx_round(2)
    lax.fori_loop(2, 4, dw_send, 0)
    y_part(-3, 0)
    dw_sum(0)
    dx_round(3)
    dw_sum(1)
    dx_terms(6)
    dw_sum(2)
    dx_round(4)
    dw_sum(3)
    dx_terms(7)
    y_part(-4, 0)
    y_part(3, 0)
    dx_round(5)

    mine = c * 32 + x * 8 + zh * 2
    for j in (1, 2, 0):
        part = zrb.at[j]
        remote(part, part, wzs.at[j], wzr.at[j], core).wait_recv()
    for i in range(2):
        total = wf[i]
        for j in range(3):
            total = total + decode(zrb.at[j, i])
        total = jnp.where(mine + i < table_ref[192], total.T, jnp.zeros((BLK, BLK), F32))
        bg_ref[mine + i] = total.astype(BF16)

    def slots(dx, dzh, n=2, half=c):
        return bg_ref.at[pl.ds(half * 32 + lax.rem(x + dx + NX, NX) * 8 + lax.rem(zh + dzh + NZH, NZH) * 2, n)]

    def put(part, ss, rs, dev):
        copy = remote(part, part, ss, rs, dev)
        copy.start()
        sent.append(copy)

    def over(m, k):
        put(slots((0, -1, 1, 2)[m], -k), gcs.at[m, k], gcr.at[m, k], core)

    def gx_send(k):
        for way in (0, 1):
            put(slots(0, -k), gxs.at[way, k], gxr.at[way, k], xp if way == 0 else xm)

    def gx_pass(k):
        for way, dx in ((0, -1), (1, 1)):
            part = slots(dx, -k)
            remote(part, part, gxs.at[way, k], gxr.at[way, k], core).wait_recv()
            if (k in (0, 1)) == (way == 0):
                put(part, gfs.at[k], gfr.at[k], xp if way == 0 else xm)
            over(1 + way, k)

    def gf_take(k):
        part = slots(2, -k)
        remote(part, part, gfs.at[k], gfr.at[k], core).wait_recv()
        over(3, k)

    for k in (2, 1, 3):
        put(slots(0, 0), gzs.at[k], gzr.at[k], zhs[k])
    gx_send(0)
    over(0, 0)
    for copy in sent[:from_gather]:
        copy.wait_send()
    dx_round(6)
    for k in (1, 3, 2):
        part = slots(0, -k)
        remote(part, part, gzs.at[k], gzr.at[k], core).wait_recv()
        gx_send(k)
        over(0, k)
        if k == 1:
            gx_pass(0)

    def z_copy(j):
        return remote(dxb.at[1 - zl, 0, j], dxz.at[j], dzs.at[j], dzr.at[j], zp)

    for way in (0, 1):
        for j in range(SUB):
            dx_copy(way, 0, j).wait_send()
    for j in range(SUB):
        for way in (0, 1):
            dxf[way, j] = dx_part(way, 7, j)
        encode(dxb.at[1 - zl, 0, j], dxf[1 - zl, j])
        z_copy(j).start()
    gx_pass(1)
    gx_pass(3)
    y_part(-2, 1)
    y_part(2, 1)
    gx_pass(2)
    y_part(-3, 1)
    y_part(3, 1)
    y_part(-4, 1)
    y_ref[...] = yacc[...].astype(BF16)
    for j in range(SUB):
        part = dxz.at[j]
        remote(part, part, dzs.at[j], dzr.at[j], core).wait_recv()
        dx_ref[:, j * BLK : (j + 1) * BLK] = (dxf[zl, j] + decode(part)).astype(BF16)
    for j in range(3):
        wz_copy(j).wait_send()

    for way in (0, 1):

        def left(n, carry, way=way):
            dx_copy(way, lax.div(n, SUB), lax.rem(n, SUB)).wait_send()
            return carry

        lax.fori_loop(SUB, 7 * SUB, left, 0)
    for o in range(3):

        def gone(j, carry, o=o):
            dw_copy(o, j).wait_send()
            return carry

        lax.fori_loop(0, 4, gone, 0)

    for k in (0, 1, 3, 2):
        gf_take(k)
    for m in range(4):
        for k in range(4):
            part = slots((0, -1, 1, 2)[m], -k, 2, 1 - c)
            remote(part, part, gcs.at[m, k], gcr.at[m, k], core).wait_recv()

    for copy in sent[from_gather:]:
        copy.wait_send()
    for j in range(SUB):
        z_copy(j).wait_send()


def per_device(tokens, cotangent, blocks, slot_block, shard_count):
    n = jnp.arange(193, dtype=jnp.int32)[:, None]
    place = jnp.arange(64, dtype=jnp.int32)[None, :]
    block = n // 2 * 32 + lax.axis_index("fsdp") * 2 + n % 2
    held = (slot_block[None, :] == block) & (place < shard_count[0])
    entry = jnp.where(n < 128, jnp.where(held, place, -1), jnp.where(place == n - 128, slot_block[None, :], -1))
    table = jnp.max(jnp.where(n < 192, entry, shard_count[0]), axis=1)
    smem, vmem, hbm = (pl.BlockSpec(memory_space=m) for m in (pltpu.SMEM, pltpu.VMEM, pltpu.HBM))
    dma = pltpu.SemaphoreType.DMA
    return pl.pallas_call(
        kernel,
        out_shape=(
            jax.ShapeDtypeStruct((TOK, CF), BF16),
            jax.ShapeDtypeStruct((TOK, XF), BF16),
            jax.ShapeDtypeStruct((64, BLK, BLK), BF16),
        ),
        in_specs=[smem] + [hbm] * 3,
        out_specs=(vmem,) * 3,
        scratch_shapes=[
            pltpu.VMEM((64, 2 * TOK, BLK), BF16),
            pltpu.VMEM((2 * TOK, CF), BF16),
            pltpu.VMEM((2, BLK, 2 * TOK), BF16),
            pltpu.VMEM((64, BLK, BLK), BF16),
            pltpu.VMEM((64 * BLK, CF), BF16),
            pltpu.VMEM((TOK, CF), F32),
            pltpu.VMEM((2, 8, SUB, BLK, BLK), F32),
            pltpu.VMEM((2, 8, SUB, CODE, BLK), jnp.int32),
            pltpu.VMEM((2, SUB, BLK, BLK), F32),
            pltpu.VMEM((SUB, CODE, BLK), jnp.int32),
            pltpu.VMEM((3, 4, 2, CODE, BLK), jnp.int32),
            pltpu.VMEM((3, 4, 2, CODE, BLK), jnp.int32),
            pltpu.VMEM((2, BLK, BLK), F32),
            pltpu.VMEM((3, 2, CODE, BLK), jnp.int32),
            pltpu.VMEM((3, 2, CODE, BLK), jnp.int32),
            dma((6,)), dma((40,)), dma((40,)), dma((17,)), dma((17,)),
            dma((2, 8, SUB)), dma((2, 8, SUB)), dma((SUB,)), dma((SUB,)),
            dma((3, 4)), dma((3, 4)), dma((3,)), dma((3,)),
            dma((4,)), dma((4,)), dma((2, 4)), dma((2, 4)), dma((4,)), dma((4,)), dma((4, 4)), dma((4, 4)),
        ],
        compiler_params=pltpu.CompilerParams(
            collective_id=0, has_side_effects=True, vmem_limit_bytes=50 << 20
        ),
    )(table, tokens, cotangent, blocks)


def solution(mesh):
    return jax.shard_map(
        per_device,
        mesh=mesh,
        in_specs=(P("dp", "fsdp"), P("dp", "fsdp"), P("fsdp", None, None), P("fsdp"), P("fsdp")),
        out_specs=(P("dp", "fsdp"), P("dp", "fsdp"), P("fsdp", None, None)),
        check_vma=False,
    )
```
